128 devices in a mesh: row: 16 (over z, x), col: 8 (over y, core).
Axes of the slice: x: 4, y: 4, z: 4, core: 2. Of those that a mesh axis runs over, the one named last changes fastest.
Arguments:
- front: float32 [4, 4096, 8, 2048], P(None, 'row', None, 'col'), may hold values from -1 to 64, as said below
- child_blocks: float32 [1024, 256, 256], P(('row', 'col')), may hold values from -4 to 4
- child_rows: int32 [1024, 256], P(('row', 'col')), may hold values from 512 to 16383, as said below
- child_cols: int32 [1024, 256], P(('row', 'col')), may hold values from 512 to 16383, as said below
- child_count: int32 [128], P(('row', 'col')), may hold values from 5 to 8, as said below
Outputs:
- factored: float32 [4, 4096, 8, 2048], P(None, 'row', None, 'col')
The draws below stay inside these ranges and needn't reach their ends.
Inputs may be any that keep to these rules, and one draw needn't show every extreme that they name: `front`: the first 512 diagonal entries lie in [32, 64]; every other entry lies in [-1, 1]. `child_rows`: all 256 rows of one child block land in one block row of index 2 or more whose index modulo 16 is the row index of the device that holds the block; positions within it may repeat. `child_cols`: all 256 columns of one child block land in one block column of index 2 or more; among the live blocks of one device at most 2 land in block columns of one device column (block column modulo 8), and on every device some device column gets exactly 2. `child_count`: some device has all 8 blocks live.
All inputs are finite; a program needn't handle non-finite values.
Results may differ from the reference program's by a relative error of at most 0.0001.
Values sent between devices are 32-bit elements; how exact they have to be, the bound alone decides.
A program may use at most 128 MiB of HBM per device.

```python
import jax
import jax.numpy as jnp
from jax import lax

B = 256
BRD = 4
CB = 8
CAP = 2
PANELS = 2
BCD = 8
CHILDREN = 1024
N_ROW = 16
N_COL = 8
DEVICES = 128


def draw_front(key, part):
    key = jax.random.fold_in(key, 11)
    order_total = BRD * N_ROW * B
    key_off, key_diag = jax.random.split(key, 2)
    spread = jnp.clip(jax.random.normal(key_off, (order_total, order_total)) * 0.5, -1.0, 1.0)
    diag_values = jax.random.uniform(key_diag, (order_total, 1), minval=32.0, maxval=64.0)
    positions = jnp.arange(order_total)
    pivot_diag = (positions[:, None] == positions[None, :]) & (positions[:, None] < PANELS * B)
    matrix = jnp.where(pivot_diag, diag_values, spread).astype(jnp.float32)
    return matrix.reshape(BRD, N_ROW * B, -1, N_COL * B)


def draw_child_rows(key, part):
    key = jax.random.fold_in(key, 23)
    total = DEVICES * CB
    key_first, key_later, key_offset = jax.random.split(key, 3)
    device = jnp.arange(total, dtype=jnp.int32) // CB
    dev_row = device // N_COL
    first = jax.random.randint(key_first, (total,), 0, BRD)
    later = jax.random.randint(key_later, (total,), 1, BRD)
    block_row = first * N_ROW + dev_row
    block_row = jnp.where(block_row < PANELS, later * N_ROW + dev_row, block_row)
    offsets = jax.random.randint(key_offset, (total, B), 0, B)
    return (block_row[:, None] * B + offsets).astype(jnp.int32)


def draw_child_cols(key, part):
    key = jax.random.fold_in(key, 37)
    total = DEVICES * CB
    key_perm, key_shift, key_first, key_later, key_offset = jax.random.split(key, 5)
    slot_total = N_COL * CAP
    perm_keys = jax.random.split(key_perm, DEVICES)
    orders = jax.vmap(lambda single: jax.random.permutation(single, slot_total - CAP))(perm_keys) + CAP
    leading = jnp.broadcast_to(jnp.arange(CAP, dtype=jnp.int32)[None, :], (DEVICES, CAP))
    sequence = jnp.concatenate([leading, orders.astype(jnp.int32)], axis=1)[:, :CB]
    shift = jax.random.randint(key_shift, (DEVICES, 1), 0, N_COL)
    owners = ((sequence // CAP + shift) % N_COL).reshape(total)
    first = jax.random.randint(key_first, (total,), 0, BCD)
    later = jax.random.randint(key_later, (total,), 1, BCD)
    block_col = first * N_COL + owners
    block_col = jnp.where(block_col < PANELS, later * N_COL + owners, block_col)
    offsets = jax.random.randint(key_offset, (total, B), 0, B)
    return (block_col[:, None] * B + offsets).astype(jnp.int32)


def draw_child_count(key, part):
    key = jax.random.fold_in(key, 53)
    key_count, key_full = jax.random.split(key)
    counts = jax.random.randint(key_count, (DEVICES,), CB // 2 + 1, CB + 1)
    full_device = jax.random.randint(key_full, (), 0, DEVICES)
    return jnp.where(jnp.arange(DEVICES) == full_device, CB, counts).astype(jnp.int32)


def levels(key, shape, cuts, smallest, high):
    level, own = 1.0, jax.random.fold_in(key, 6)
    for position, shards_of in cuts:
        heights = jnp.exp(jax.random.uniform(jax.random.fold_in(own, position), (shards_of,), jnp.float32, smallest / len(cuts), high / len(cuts)))
        level = level * jnp.repeat(heights, shape[position] // shards_of).reshape([-1 if axis == position else 1 for axis in range(len(shape))])
    return level


def gaussian(own_key, dims, scale, limit, shards=(), kind=jnp.bfloat16):
    result = jax.random.normal(own_key, dims, jnp.float32) * scale
    if len(shards) > 0:
        result = levels(own_key, dims, shards, -0.22, 0.18) * result
    return jnp.clip(result, min=-limit, max=limit).astype(kind)


def setup_inputs(seed: int = 0) -> dict:
    seeds = jax.random.split(jax.random.key(seed), 6)
    return {
        "front": draw_front(jax.random.fold_in(seeds[5], 71), 0),
        "child_blocks": gaussian(seeds[1], (CHILDREN, B, B), 1.0, 4.0, ((0, 128),), jnp.float32),
        "child_rows": draw_child_rows(jax.random.fold_in(seeds[5], 71), 0),
        "child_cols": draw_child_cols(jax.random.fold_in(seeds[5], 71), 0),
        "child_count": draw_child_count(jax.random.fold_in(seeds[5], 71), 0),
    }


def reference(front, child_blocks, child_rows, child_cols, child_count):
    order_total = BRD * N_ROW * B
    matrix = front.reshape(order_total, order_total)
    slot_index = jnp.arange(DEVICES * CB, dtype=jnp.int32) % CB
    live_scale = (slot_index < jnp.repeat(child_count, CB)).astype(jnp.float32)
    matrix = matrix.at[child_rows[:, :, None], child_cols[:, None, :]].add(child_blocks * live_scale[:, None, None])
    block_of = jnp.arange(order_total, dtype=jnp.int32) // B
    for panel in range(PANELS):
        column = matrix[:, panel * B:(panel + 1) * B]
        pivot_block = column[panel * B:(panel + 1) * B]
        diag_factor = jnp.linalg.cholesky((pivot_block + pivot_block.T) * 0.5)
        solved = lax.linalg.triangular_solve(diag_factor, column, left_side=False, lower=True, transpose_a=True)
        lower_part = jnp.where(block_of[:, None] > panel, solved, jnp.float32(0.0))
        matrix = matrix - jnp.dot(lower_part, lower_part.T, precision=lax.Precision.HIGHEST)
        panel_block = lower_part.at[panel * B:(panel + 1) * B].set(diag_factor)
        matrix = matrix.at[:, panel * B:(panel + 1) * B].set(panel_block)
        matrix = matrix.at[panel * B:(panel + 1) * B, (panel + 1) * B:].set(jnp.float32(0.0))
    return matrix.reshape(front.shape)
```

```python
import functools

import jax
import jax.numpy as jnp
from jax import lax
from jax.experimental import pallas as pl
from jax.experimental.pallas import tpu as pltpu
from jax.sharding import PartitionSpec as P

F32 = jnp.float32
BF = jnp.bfloat16
MESH = pl.DeviceIdType.MESH
TN = (((0,), (0,)), ((), ()))
NT = (((1,), (1,)), ((), ()))
NN = (((1,), (0,)), ((), ()))


def hdot(a, b, dn):
    return lax.dot_general(a, b, dn, precision=lax.Precision.HIGHEST, preferred_element_type=F32)


def bdot(a, b, dn):
    return lax.dot_general(a, b, dn, preferred_element_type=F32)


def split(x):
    hi = x.astype(BF)
    return hi, (x - hi.astype(F32)).astype(BF)


def factor(A, group=8, strip=32):
    ns = 128//strip
    lane = lax.broadcasted_iota(jnp.int32,(strip,128),1)
    sub = lax.broadcasted_iota(jnp.int32,(strip,128),0)
    def tile(J,carry):
        c0 = pl.multiple_of(J*128,128)
        for t in range(ns):
            r0 = pl.multiple_of(c0+strip*t,strip)
            S = [A[pl.ds(r0,strip),128*i:128*i+128] for i in range(4)]
            T = A[pl.ds(r0,strip),pl.ds(c0,128)]
            for s0 in range(0,strip,group):
                cols=[jnp.broadcast_to(T[:,strip*t+s0+a:strip*t+s0+a+1],(strip,128)) for a in range(group)]
                fs=[]
                for a in range(group):
                    s=s0+a
                    rd=1.0/cols[a][s:s+1,:]
                    f=jnp.where(sub>s,cols[a]*rd,0.0)
                    fs.append(f)
                    for b in range(a+1,group):
                        cols[b]=cols[b]-f*cols[b][s:s+1,:]
                for a in range(group):
                    s=s0+a; k=strip*t+s
                    f=fs[a]
                    rowT=jnp.where(lane[:1]==k,1.0,T[s:s+1,:])
                    T=jnp.where((lane==k)&(sub>s),0.0,T)-f*rowT
                    S=[x-f*x[s:s+1,:] for x in S]
            dg=(lane==sub+strip*t)
            d=jnp.sum(jnp.where(dg,T,0.0),axis=1,keepdims=True)
            rs=lax.rsqrt(d)
            rs=rs*(1.5-0.5*d*rs*rs)
            rs=jnp.broadcast_to(rs,(strip,128))
            T=jnp.where(dg,1.0,T)*rs
            for i in range(4): A[pl.ds(r0,strip),128*i:128*i+128]=S[i]*rs
            if t<ns-1:
                n=128-strip*(t+1)
                A[pl.ds(r0,strip),pl.ds(c0,128)]=jnp.where((lane>sub+strip*t)&(lane<strip*(t+1)),0.0,T)
                R=A[pl.ds(r0,strip),:]
                lm=jnp.where(lane>=strip*(t+1),T,0.0)
                upd=hdot(lm,R,TN)
                rb=pl.multiple_of(r0+strip,strip)
                lane_n=lax.broadcasted_iota(jnp.int32,(n,128),1)
                Tt=A[pl.ds(rb,n),pl.ds(c0,128)]
                A[pl.ds(rb,n),pl.ds(c0,128)]=jnp.where((lane_n>=strip*t)&(lane_n<strip*(t+1)),0.0,Tt)
                A[pl.ds(rb,n),:]=A[pl.ds(rb,n),:]-upd[strip*(t+1):]
            A[pl.ds(r0,strip),pl.ds(c0,128)]=T
        R=A[pl.ds(c0,128),:]
        D=A[pl.ds(c0,128),pl.ds(c0,128)]
        i1=lax.broadcasted_iota(jnp.int32,(128,128),1); i0=lax.broadcasted_iota(jnp.int32,(128,128),0)
        D=jnp.where(i1>i0,0.0,D)
        for m in range(1,4):
            @pl.when(m>J)
            def _(m=m):
                lm=A[pl.ds(c0,128),m*128:(m+1)*128]
                A[m*128:(m+1)*128,:]=A[m*128:(m+1)*128,:]-hdot(lm,R,TN)
                A[m*128:(m+1)*128,pl.ds(c0,128)]=-hdot(lm,D,TN)
        return carry
    lax.fori_loop(0,4,tile,0)


def m4(v):
    return lax.rem(v + 8, 4)


def comm_kernel(
    pan, cb, crow, ccol, crow_s, ccol_s, cnt_s,
    recv, lrh, lrl, lch, lcl, corner,
    stage, PR, PC, DG, AW, Wh, Wl, oh, ol,
    h0, h1, h2, h3, h4, h5, y0s, y0r, y1s, y1r, ds, dr, dloc, xs_, xr_, cs, cr, osem,
):
    r = lax.axis_index("row")
    c = lax.axis_index("col")
    z, x = r // 4, lax.rem(r, 4)
    y, k = c // 2, lax.rem(c, 2)

    def dev(z, x, y, k):
        return (z * 4 + x, y * 2 + k)

    other = dev(z, x, y, 1 - k)
    b = pltpu.get_barrier_semaphore()
    for d in range(1, 8):
        pl.semaphore_signal(b, inc=1, device_id=(r, lax.rem(c + d, 8)), device_id_type=MESH)
    for s in (1, 3):
        pl.semaphore_signal(b, inc=1, device_id=dev(z, m4(x + s), y, k), device_id_type=MESH)
        pl.semaphore_signal(b, inc=1, device_id=dev(m4(z + s), x, y, k), device_id_type=MESH)
    pl.semaphore_wait(b, 11)

    def rcopy(src, dst, ss, rs, to):
        return pltpu.make_async_remote_copy(
            src_ref=src, dst_ref=dst, send_sem=ss, recv_sem=rs, device_id=to, device_id_type=MESH
        )

    def pack():
        owner = [lax.rem(ccol_s[s, 0] // 256, 8) for s in range(8)]
        live = [(s < cnt_s[0]).astype(jnp.int32) for s in range(8)]
        rank = []
        for s in range(8):
            n = jnp.int32(0)
            for q in range(s):
                n = n + live[q] * (owner[q] == owner[s]).astype(jnp.int32)
            rank.append(n)

        def slot(t, carry):
            idx = jnp.int32(0)
            ok = jnp.int32(0)
            for s in range(8):
                hit = live[s] * (owner[s] * 2 + rank[s] == t).astype(jnp.int32)
                idx = idx + hit * s
                ok = ok + hit
            rows = crow[pl.ds(idx, 1), :]
            cols = ccol[pl.ds(idx, 1), :]
            brow = rows // 4096
            bcol = cols // 2048
            code = jnp.where(ok > 0, brow * 8 + bcol, -1)
            stage[t, 0:256, :] = cb[idx]
            stage[t, 256:257, :] = lax.rem(rows, 256).astype(F32)
            stage[t, 257:258, :] = lax.rem(cols, 256).astype(F32)
            stage[t, 258:259, :] = code.astype(F32)
            stage[t, 259:264, :] = jnp.zeros((5, 256), F32)
            return carry

        lax.fori_loop(0, 16, slot, 0)

    def child_copy(d):
        to = lax.rem(c + d, 8)
        return rcopy(
            stage.at[pl.ds(to * 2, 2)], recv.at[pl.ds(c * 2, 2)], cs.at[d], cr.at[d], (r, to)
        )

    own_copy = pltpu.make_async_copy(stage.at[pl.ds(c * 2, 2)], recv.at[pl.ds(c * 2, 2)], cs.at[0])

    def start_children():
        own_copy.start()
        for d in (1, 7, 2, 6, 3, 5, 4):
            child_copy(d).start()

    def wait_children():
        own_copy.wait()
        for d in range(1, 8):
            child_copy(d).wait()

    def tree(src_z, src_x, xfirst, s1, s2, make):
        oz, ox = z - src_z, x - src_x
        a = m4(s1 * jnp.where(xfirst == 1, ox, oz))
        bb = m4(s2 * jnp.where(xfirst == 1, oz, ox))
        dz1, dx1 = jnp.where(xfirst == 1, 0, s1), jnp.where(xfirst == 1, s1, 0)
        dz2, dx2 = jnp.where(xfirst == 1, s2, 0), jnp.where(xfirst == 1, 0, s2)
        is_src = jnp.logical_and(a == 0, bb == 0)
        conds = (
            jnp.logical_and(bb == 0, a <= 1),
            jnp.logical_and(bb == 0, a == 0),
            bb <= 1,
            bb == 0,
        )
        targets = (
            dev(m4(z + dz1), m4(x + dx1), y, k),
            dev(m4(z - dz1), m4(x - dx1), y, k),
            dev(m4(z + dz2), m4(x + dx2), y, k),
            dev(m4(z - dz2), m4(x - dx2), y, k),
        )
        copies = [make(e, to) for e, to in enumerate(targets)]
        return is_src, conds, copies

    h0_copy = rcopy(pan.at[pl.ds(1, 3)], PR.at[0, pl.ds(1, 3)], h0.at[0], h0.at[1], other)
    h1_copy = rcopy(pan.at[0], PR.at[1, 0], h1.at[0], h1.at[1], other)
    h2_copy = [
        rcopy(PR.at[p, 0], PR.at[p, 0], h2.at[p, 0], h2.at[p, 1], other) for p in range(2)
    ]
    h3_copy = rcopy(AW, AW, h3.at[0], h3.at[1], other)

    def h4_copy(j):
        p, br = lax.rem(j, 2), 1 + j // 2
        return rcopy(PR.at[p, br], PR.at[p, br], h4.at[j, 0], h4.at[j, 1], other)

    def xz_index(q):
        i, s = q // 4, lax.rem(q, 4)
        return lax.rem(s, 2), s // 2, lax.rem(i, 2), lax.rem(i // 2 + 1, 4)

    def h5_copy(q):
        kk, src, p, br = xz_index(q)
        ref = PC.at[kk, src, p, br]
        return rcopy(ref, ref, h5.at[q, 0], h5.at[q, 1], other)

    def y0_parts(j):
        p, qt = j // 4, lax.rem(j, 4)
        s = 1 - 2 * p
        yy = m4(s * y)
        ref = PR.at[p, 0, pl.ds(qt * 64, 64)]
        fwd = rcopy(ref, ref, y0s.at[j, 0], y0r.at[j], dev(z, x, m4(y + s), k))
        back = rcopy(ref, ref, y0s.at[j, 1], y0r.at[j], dev(z, x, m4(y - s), k))
        return yy, fwd, back

    def d_parts(j):
        d, qt = j // 4, lax.rem(j, 4)
        rows = pl.ds(qt * 64, 64)
        ref = DG.at[d, rows]
        src_x = jnp.minimum(d, 1)
        s1 = 1 - 2 * lax.rem(d, 2)
        parts = tree(
            0, src_x, 1, s1, s1, lambda e, to: rcopy(ref, ref, ds.at[j, e], dr.at[j], to)
        )
        return parts, d, rows

    @pl.when(k == 0)
    def _():
        @pl.when(y == 0)
        def _():
            h0_copy.start()
            PR[0, 0] = pan[0]

        def y0_step(j, carry):
            yy, fwd, back = y0_parts(j)

            @pl.when(yy != 0)
            def _():
                fwd.wait_recv()

            @pl.when(jnp.logical_and(yy == 0, j == 4))
            def _():
                h1_copy.wait_recv()

            @pl.when(yy <= 1)
            def _():
                fwd.start()

            @pl.when(yy == 0)
            def _():
                back.start()

            return carry

        lax.fori_loop(0, 8, y0_step, 0)
        for p in range(2):
            h2_copy[p].start()

        def d_step(j, carry):
            (is_src, conds, copies), d, rows = d_parts(j)

            @pl.when(is_src)
            def _():
                DG[d, rows, :] = PR[d // 2, 0, rows, :]

            @pl.when(jnp.logical_not(is_src))
            def _():
                copies[0].wait_recv()

            for cond, cp in zip(conds, copies):
                @pl.when(cond)
                def _(cp=cp):
                    cp.start()

            return carry

        lax.fori_loop(0, 12, d_step, 0)
        pack()
        start_children()

        AW[0:256, 0:256] = (DG[0] + DG[0].T) * 0.5
        AW[0:256, 256:512] = DG[1].T
        AW[256:512, 0:256] = jnp.zeros((256, 256), F32)
        AW[256:512, 256:512] = (DG[2] + DG[2].T) * 0.5
        factor(AW)
        h3_copy.start()

        def h4_wait(j, carry):
            h4_copy(j).wait_recv()
            return carry

        lax.fori_loop(0, 6, h4_wait, 0)

        def h5_wait(q, carry):
            @pl.when(lax.rem(q, 2) == 0)
            def _():
                h5_copy(q).wait_recv()

            return carry

        lax.fori_loop(0, 32, h5_wait, 0)

    def y1_parts(j):
        p, br = lax.rem(j, 2), 1 + j // 2
        s = 1 - 2 * p
        yy = m4(s * y)
        ref = PR.at[p, br]
        return yy, rcopy(ref, ref, y1s.at[j], y1r.at[j], dev(z, x, m4(y + s), k))

    def xz_parts(q):
        kk, src, p, br = xz_index(q)
        i = q // 4
        row = 2 * y + kk + 8 * src
        ref = PC.at[kk, src, p, br]
        xfirst = lax.rem(i, 2)
        s1 = 1 - 2 * lax.rem(i // 2, 2)
        s2 = 1 - 2 * lax.rem(i // 4, 2)
        return tree(
            row // 4, lax.rem(row, 4), xfirst, s1, s2,
            lambda e, to: rcopy(ref, ref, xs_.at[q, e], xr_.at[q], to),
        )

    @pl.when(k == 1)
    def _():
        @pl.when(y == 0)
        def _():
            PR[1, 1:4] = pan[1:4]
            h1_copy.start()
            h0_copy.wait_recv()

        def y1_step(j, carry):
            yy, fwd = y1_parts(j)

            @pl.when(yy != 0)
            def _():
                fwd.wait_recv()

            @pl.when(yy < 3)
            def _():
                fwd.start()

            h4_copy(j).start()
            return carry

        lax.fori_loop(0, 6, y1_step, 0)
        pack()
        start_children()
        for p in range(2):
            h2_copy[p].wait_recv()

        def xz_step(q, carry):
            is_src, conds, copies = xz_parts(q)
            kk, src, p, br = xz_index(q)

            @pl.when(is_src)
            def _():
                PC[kk, src, p, br] = PR[p, br]

            @pl.when(jnp.logical_not(is_src))
            def _():
                copies[0].wait_recv()

            for cond, cp in zip(conds, copies):
                @pl.when(cond)
                def _(cp=cp):
                    cp.start()

            @pl.when(kk == 0)
            def _():
                h5_copy(q).start()

            return carry

        lax.fori_loop(0, 32, xz_step, 0)
        h3_copy.wait_recv()

    i0 = lax.broadcasted_iota(jnp.int32, (256, 256), 0)
    i1 = lax.broadcasted_iota(jnp.int32, (256, 256), 1)
    low = i1 <= i0
    Wh[0], Wl[0] = split(jnp.where(low, AW[0:256, 0:256], 0.0))
    Wh[1], Wl[1] = split(AW[256:512, 0:256])
    Wh[2], Wl[2] = split(jnp.where(low, AW[256:512, 256:512], 0.0))

    def times_w(h, l, w):
        return bdot(h, Wh[w], NT) + (bdot(h, Wl[w], NT) + bdot(l, Wh[w], NT))

    def solve(m0, m1, put):
        h0_, l0_ = split(m0)
        h1_, l1_ = split(m1)
        a = times_w(h0_, l0_, 0)
        put(0, *split(a))
        e = times_w(h0_, l0_, 1) + times_w(h1_, l1_, 2)
        put(1, *split(e))

    def row_solve(i, carry):
        def put(p, hi, lo):
            oh[i, :, pl.ds(p * 256, 256)] = hi
            ol[i, :, pl.ds(p * 256, 256)] = lo

        solve(PR[0, i], PR[1, i], put)
        return carry

    lax.fori_loop(0, 4, row_solve, 0)

    def col_solve(i, carry):
        def put(p, hi, lo):
            oh[4 + i, :, pl.ds(p * 256, 256)] = hi
            ol[4 + i, :, pl.ds(p * 256, 256)] = lo

        solve(PC[k, lax.rem(i, 2), 0, i // 2], PC[k, lax.rem(i, 2), 1, i // 2], put)
        return carry

    lax.fori_loop(0, 8, col_solve, 0)
    outs = [
        pltpu.make_async_copy(oh.at[pl.ds(0, 4)], lrh, osem.at[0]),
        pltpu.make_async_copy(ol.at[pl.ds(0, 4)], lrl, osem.at[1]),
        pltpu.make_async_copy(oh.at[pl.ds(4, 8)], lch, osem.at[2]),
        pltpu.make_async_copy(ol.at[pl.ds(4, 8)], lcl, osem.at[3]),
    ]
    for cp in outs:
        cp.start()

    corner[...] = jnp.zeros((256, 256), F32)

    def diag_block(o):
        t = AW[o : o + 256, o : o + 256].T
        return jnp.where(i1 < i0, t, jnp.where(i1 == i0, 1.0 / t, 0.0))

    @pl.when(jnp.logical_and(r == 0, c == 0))
    def _():
        corner[...] = diag_block(0)

    @pl.when(jnp.logical_and(r == 1, c == 0))
    def _():
        corner[...] = AW[0:256, 256:512].T

    @pl.when(jnp.logical_and(r == 1, c == 1))
    def _():
        corner[...] = diag_block(256)

    @pl.when(k == 0)
    def _():
        @pl.when(y == 0)
        def _():
            h0_copy.wait_send()

        def y0_end(j, carry):
            yy, fwd, back = y0_parts(j)

            @pl.when(yy <= 1)
            def _():
                fwd.wait_send()

            @pl.when(yy == 0)
            def _():
                back.wait_send()

            return carry

        lax.fori_loop(0, 8, y0_end, 0)
        for p in range(2):
            h2_copy[p].wait_send()

        def d_end(j, carry):
            (is_src, conds, copies), d, rows = d_parts(j)
            for cond, cp in zip(conds, copies):
                @pl.when(cond)
                def _(cp=cp):
                    cp.wait_send()

            return carry

        lax.fori_loop(0, 12, d_end, 0)
        h3_copy.wait_send()

    @pl.when(k == 1)
    def _():
        @pl.when(y == 0)
        def _():
            h1_copy.wait_send()

        def y1_end(j, carry):
            yy, fwd = y1_parts(j)

            @pl.when(yy < 3)
            def _():
                fwd.wait_send()

            h4_copy(j).wait_send()
            return carry

        lax.fori_loop(0, 6, y1_end, 0)

        def xz_end(q, carry):
            is_src, conds, copies = xz_parts(q)
            for cond, cp in zip(conds, copies):
                @pl.when(cond)
                def _(cp=cp):
                    cp.wait_send()

            @pl.when(lax.rem(q, 2) == 0)
            def _():
                h5_copy(q).wait_send()

            return carry

        lax.fori_loop(0, 32, xz_end, 0)

    wait_children()
    for cp in outs:
        cp.wait()


def exchange(pan, child_blocks, child_rows, child_cols, child_count):
    vm = pl.BlockSpec(memory_space=pltpu.VMEM)
    sm = pl.BlockSpec(memory_space=pltpu.SMEM)
    hbm = pl.BlockSpec(memory_space=pl.ANY)
    dma = pltpu.SemaphoreType.DMA
    return pl.pallas_call(
        comm_kernel,
        out_shape=(
            jax.ShapeDtypeStruct((16, 264, 256), F32),
            jax.ShapeDtypeStruct((4, 256, 512), BF),
            jax.ShapeDtypeStruct((4, 256, 512), BF),
            jax.ShapeDtypeStruct((8, 256, 512), BF),
            jax.ShapeDtypeStruct((8, 256, 512), BF),
            jax.ShapeDtypeStruct((256, 256), F32),
        ),
        in_specs=[vm, vm, vm, vm, sm, sm, sm],
        out_specs=(hbm, hbm, hbm, hbm, hbm, vm),
        scratch_shapes=[
            pltpu.VMEM((16, 264, 256), F32),
            pltpu.VMEM((2, 4, 256, 256), F32),
            pltpu.VMEM((2, 2, 2, 4, 256, 256), F32),
            pltpu.VMEM((3, 256, 256), F32),
            pltpu.VMEM((512, 512), F32),
            pltpu.VMEM((3, 256, 256), BF),
            pltpu.VMEM((3, 256, 256), BF),
            pltpu.VMEM((12, 256, 512), BF),
            pltpu.VMEM((12, 256, 512), BF),
            dma((2,)), dma((2,)), dma((2, 2)), dma((2,)), dma((6, 2)), dma((32, 2)),
            dma((8, 2)), dma((8,)), dma((6,)), dma((6,)),
            dma((12, 4)), dma((12,)), dma, dma((32, 4)), dma((32,)),
            dma((8,)), dma((8,)), dma((4,)),
        ],
        compiler_params=pltpu.CompilerParams(
            collective_id=1, has_side_effects=True, vmem_limit_bytes=52 << 20
        ),
        name="exchange",
    )(pan, child_blocks, child_rows, child_cols, child_rows, child_cols, child_count)


def finish(mode, front_ref, recv_ref, lrh_ref, lrl_ref, lch_ref, lcl_ref, corner_ref, out_ref, add_ref, code_ref):
    i=pl.program_id(0)
    r=lax.axis_index("row") if "nomesh" not in mode else 3
    c=lax.axis_index("col") if "nomesh" not in mode else 3
    @pl.when(i==0)
    def _():
        for s in range(16):
            code_ref[s]=jnp.max(recv_ref[s,258:259,:]).astype(jnp.int32)
    add_ref[...]=jnp.zeros_like(add_ref)
    if "noch" not in mode:
        def slot(s,carry):
            code=code_ref[s]
            @pl.when((code>>3)==i)
            def _():
                rows=recv_ref[s,256:257,:].astype(jnp.int32)
                cols=recv_ref[s,257:258,:].astype(jnp.int32)
                t=lax.broadcasted_iota(jnp.int32,(256,256),0)
                R=jnp.where(rows==t,1.0,0.0).astype(BF)
                Q=jnp.where(cols==t,1.0,0.0).astype(BF)
                h,l=split(recv_ref[s,0:256,:])
                p=bdot(R,h,NN)+bdot(R,l,NN)
                h,l=split(p)
                j=code&7
                add_ref[j]=add_ref[j]+(bdot(h,Q,NT)+bdot(l,Q,NT))
            return carry
        lax.fori_loop(0,16,slot,0)
    special=jnp.logical_and(i==0,r<2)
    ah=lrh_ref[0]; al=lrl_ref[0]
    for j in range(8):
        bh=lch_ref[j]; bl=lcl_ref[j]
        if "noup" in mode: u=0.0
        else: u=bdot(ah,bh,NT)+(bdot(ah,bl,NT)+bdot(al,bh,NT))
        v=front_ref[0,:,j,:]+add_ref[j]-u
        out_ref[0,:,j,:]=v
    @pl.when(c<2)
    def _():
        @pl.when(c==0)
        def _(): out_ref[0,:,0,:]=ah[:,0:256].astype(F32)+al[:,0:256].astype(F32)
        @pl.when(c==1)
        def _(): out_ref[0,:,0,:]=ah[:,256:512].astype(F32)+al[:,256:512].astype(F32)
    @pl.when(special)
    def _():
        out_ref[0,:,1:8,:]=jnp.zeros((256,7,256),F32)
        out_ref[0,:,0,:]=corner_ref[...]
def kernel_b(mode,front,recv,lrh,lrl,lch,lcl,corner):
    return pl.pallas_call(functools.partial(finish,mode),grid=(4,),
        out_shape=jax.ShapeDtypeStruct((4,256,8,256),F32),
        in_specs=[pl.BlockSpec((1,256,8,256),lambda i:(i,0,0,0)),
                  pl.BlockSpec((16,264,256),lambda i:(0,0,0)),
                  pl.BlockSpec((1,256,512),lambda i:(i,0,0)),pl.BlockSpec((1,256,512),lambda i:(i,0,0)),
                  pl.BlockSpec((8,256,512),lambda i:(0,0,0)),pl.BlockSpec((8,256,512),lambda i:(0,0,0)),
                  pl.BlockSpec((256,256),lambda i:(0,0))],
        out_specs=pl.BlockSpec((1,256,8,256),lambda i:(i,0,0,0)),
        scratch_shapes=[pltpu.VMEM((8,256,256),F32),pltpu.SMEM((16,),jnp.int32)],
        compiler_params=pltpu.CompilerParams(vmem_limit_bytes=48<<20),name="finish_"+mode.replace(" ","_"))(front,recv,lrh,lrl,lch,lcl,corner)


def local(front, child_blocks, child_rows, child_cols, child_count):
    pan = front[:, :, 0, :]
    recv, lrh, lrl, lch, lcl, corner = exchange(pan, child_blocks, child_rows, child_cols, child_count)
    return kernel_b("", front, recv, lrh, lrl, lch, lcl, corner)


def solution(mesh):
    placed = (
        P(None, "row", None, "col"),
        P(("row", "col"), None, None),
        P(("row", "col"), None),
        P(("row", "col"), None),
        P(("row", "col")),
    )
    return jax.shard_map(
        local, mesh=mesh, in_specs=placed, out_specs=P(None, "row", None, "col"), check_vma=False
    )
```

```python
import functools

import jax
import jax.numpy as jnp
from jax import lax
from jax.experimental import pallas as pl
from jax.experimental.pallas import tpu as pltpu
from jax.sharding import PartitionSpec as P

F32 = jnp.float32
BF = jnp.bfloat16
MESH = pl.DeviceIdType.MESH
TN = (((0,), (0,)), ((), ()))
NT = (((1,), (1,)), ((), ()))
NN = (((1,), (0,)), ((), ()))


def hdot(a, b, dn):
    return lax.dot_general(a, b, dn, precision=lax.Precision.HIGHEST, preferred_element_type=F32)


def bdot(a, b, dn):
    return lax.dot_general(a, b, dn, preferred_element_type=F32)


def split(x):
    hi = x.astype(BF)
    return hi, (x - hi.astype(F32)).astype(BF)


def factor(A, group=8, strip=32):
    ns = 128//strip
    lane = lax.broadcasted_iota(jnp.int32,(strip,128),1)
    sub = lax.broadcasted_iota(jnp.int32,(strip,128),0)
    def tile(J,carry):
        c0 = pl.multiple_of(J*128,128)
        for t in range(ns):
            r0 = pl.multiple_of(c0+strip*t,strip)
            S = [A[pl.ds(r0,strip),128*i:128*i+128] for i in range(4)]
            T = A[pl.ds(r0,strip),pl.ds(c0,128)]
            for s0 in range(0,strip,group):
                cols=[jnp.broadcast_to(T[:,strip*t+s0+a:strip*t+s0+a+1],(strip,128)) for a in range(group)]
                fs=[]
                for a in range(group):
                    s=s0+a
                    rd=1.0/cols[a][s:s+1,:]
                    f=jnp.where(sub>s,cols[a]*rd,0.0)
                    fs.append(f)
                    for b in range(a+1,group):
                        cols[b]=cols[b]-f*cols[b][s:s+1,:]
                for a in range(group):
                    s=s0+a; k=strip*t+s
                    f=fs[a]
                    rowT=jnp.where(lane[:1]==k,1.0,T[s:s+1,:])
                    T=jnp.where((lane==k)&(sub>s),0.0,T)-f*rowT
                    S=[x-f*x[s:s+1,:] for x in S]
            dg=(lane==sub+strip*t)
            d=jnp.sum(jnp.where(dg,T,0.0),axis=1,keepdims=True)
            rs=lax.rsqrt(d)
            rs=rs*(1.5-0.5*d*rs*rs)
            rs=jnp.broadcast_to(rs,(strip,128))
            T=jnp.where(dg,1.0,T)*rs
            for i in range(4): A[pl.ds(r0,strip),128*i:128*i+128]=S[i]*rs
            if t<ns-1:
                n=128-strip*(t+1)
                A[pl.ds(r0,strip),pl.ds(c0,128)]=jnp.where((lane>sub+strip*t)&(lane<strip*(t+1)),0.0,T)
                R=A[pl.ds(r0,strip),:]
                lm=jnp.where(lane>=strip*(t+1),T,0.0)
                upd=hdot(lm,R,TN)
                rb=pl.multiple_of(r0+strip,strip)
                lane_n=lax.broadcasted_iota(jnp.int32,(n,128),1)
                Tt=A[pl.ds(rb,n),pl.ds(c0,128)]
                A[pl.ds(rb,n),pl.ds(c0,128)]=jnp.where((lane_n>=strip*t)&(lane_n<strip*(t+1)),0.0,Tt)
                A[pl.ds(rb,n),:]=A[pl.ds(rb,n),:]-upd[strip*(t+1):]
            A[pl.ds(r0,strip),pl.ds(c0,128)]=T
        R=A[pl.ds(c0,128),:]
        D=A[pl.ds(c0,128),pl.ds(c0,128)]
        i1=lax.broadcasted_iota(jnp.int32,(128,128),1); i0=lax.broadcasted_iota(jnp.int32,(128,128),0)
        D=jnp.where(i1>i0,0.0,D)
        for m in range(1,4):
            @pl.when(m>J)
            def _(m=m):
                lm=A[pl.ds(c0,128),m*128:(m+1)*128]
                A[m*128:(m+1)*128,:]=A[m*128:(m+1)*128,:]-hdot(lm,R,TN)
                A[m*128:(m+1)*128,pl.ds(c0,128)]=-hdot(lm,D,TN)
        return carry
    lax.fori_loop(0,4,tile,0)


YH = 2
NH = 1


def m4(v):
    return lax.rem(v + 8, 4)


def comm_kernel(
    pan, cb, crow, ccol, crow_s, ccol_s, cnt_s,
    recv, lrh, lrl, lch, lcl, corner,
    stage, PR, PC, DG, AW, Wh, Wl, oh, ol,
    h0, h1, h2, h3, h4, h5, y0s, y0r, y1s, y1r, ds, dr, dloc, xs_, xr_, cs, cr, osem,
):
    r = lax.axis_index("row")
    c = lax.axis_index("col")
    z, x = r // 4, lax.rem(r, 4)
    y, k = c // 2, lax.rem(c, 2)

    def dev(z, x, y, k):
        return (z * 4 + x, y * 2 + k)

    other = dev(z, x, y, 1 - k)
    b = pltpu.get_barrier_semaphore()
    for d in range(1, 8):
        pl.semaphore_signal(b, inc=1, device_id=(r, lax.rem(c + d, 8)), device_id_type=MESH)
    for s in (1, 3):
        pl.semaphore_signal(b, inc=1, device_id=dev(z, m4(x + s), y, k), device_id_type=MESH)
        pl.semaphore_signal(b, inc=1, device_id=dev(m4(z + s), x, y, k), device_id_type=MESH)
    pl.semaphore_wait(b, 11)

    def rcopy(src, dst, ss, rs, to):
        return pltpu.make_async_remote_copy(
            src_ref=src, dst_ref=dst, send_sem=ss, recv_sem=rs, device_id=to, device_id_type=MESH
        )

    def pack():
        owner = [lax.rem(ccol_s[s, 0] // 256, 8) for s in range(8)]
        live = [(s < cnt_s[0]).astype(jnp.int32) for s in range(8)]
        rank = []
        for s in range(8):
            n = jnp.int32(0)
            for q in range(s):
                n = n + live[q] * (owner[q] == owner[s]).astype(jnp.int32)
            rank.append(n)

        def slot(t, carry):
            idx = jnp.int32(0)
            ok = jnp.int32(0)
            for s in range(8):
                hit = live[s] * (owner[s] * 2 + rank[s] == t).astype(jnp.int32)
                idx = idx + hit * s
                ok = ok + hit
            rows = crow[pl.ds(idx, 1), :]
            cols = ccol[pl.ds(idx, 1), :]
            brow = rows // 4096
            bcol = cols // 2048
            code = jnp.where(ok > 0, brow * 8 + bcol, -1)
            stage[t, 0:256, :] = cb[idx]
            stage[t, 256:257, :] = lax.rem(rows, 256).astype(F32)
            stage[t, 257:258, :] = lax.rem(cols, 256).astype(F32)
            stage[t, 258:259, :] = code.astype(F32)
            stage[t, 259:264, :] = jnp.zeros((5, 256), F32)
            return carry

        lax.fori_loop(0, 16, slot, 0)

    def child_copy(d):
        to = lax.rem(c + d, 8)
        return rcopy(
            stage.at[pl.ds(to * 2, 2)], recv.at[pl.ds(c * 2, 2)], cs.at[d], cr.at[d], (r, to)
        )

    own_copy = pltpu.make_async_copy(stage.at[pl.ds(c * 2, 2)], recv.at[pl.ds(c * 2, 2)], cs.at[0])

    def start_children():
        own_copy.start()
        for d in (1, 7, 2, 6, 3, 5, 4):
            child_copy(d).start()

    def wait_children():
        own_copy.wait()
        for d in range(1, 8):
            child_copy(d).wait()

    def tree(src_z, src_x, xfirst, s1, s2, make):
        oz, ox = z - src_z, x - src_x
        a = m4(s1 * jnp.where(xfirst == 1, ox, oz))
        bb = m4(s2 * jnp.where(xfirst == 1, oz, ox))
        dz1, dx1 = jnp.where(xfirst == 1, 0, s1), jnp.where(xfirst == 1, s1, 0)
        dz2, dx2 = jnp.where(xfirst == 1, s2, 0), jnp.where(xfirst == 1, 0, s2)
        is_src = jnp.logical_and(a == 0, bb == 0)
        conds = (
            jnp.logical_and(bb == 0, a <= 1),
            jnp.logical_and(bb == 0, a == 0),
            bb <= 1,
            bb == 0,
        )
        targets = (
            dev(m4(z + dz1), m4(x + dx1), y, k),
            dev(m4(z - dz1), m4(x - dx1), y, k),
            dev(m4(z + dz2), m4(x + dx2), y, k),
            dev(m4(z - dz2), m4(x - dx2), y, k),
        )
        copies = [make(e, to) for e, to in enumerate(targets)]
        return is_src, conds, copies

    h0_copy = rcopy(pan.at[pl.ds(1, 3)], PR.at[0, pl.ds(1, 3)], h0.at[0], h0.at[1], other)
    h1_copy = rcopy(pan.at[0], PR.at[1, 0], h1.at[0], h1.at[1], other)
    h2_copy = [
        rcopy(PR.at[p, 0], PR.at[p, 0], h2.at[p, 0], h2.at[p, 1], other) for p in range(2)
    ]
    h3_copy = rcopy(AW, AW, h3.at[0], h3.at[1], other)

    def h4_copy(j):
        p, br = lax.rem(j, 2), 1 + j // 2
        return rcopy(PR.at[p, br], PR.at[p, br], h4.at[j, 0], h4.at[j, 1], other)

    def xz_index(i, s):
        ii = i // NH
        rows = pl.ds(lax.rem(i, NH) * (256 // NH), 256 // NH)
        return lax.rem(s, 2), s // 2, lax.rem(ii, 2), lax.rem(ii // 2 + 1, 4), rows

    def h5_copy(i, src):
        kk, src, p, br, rows = xz_index(i, 2 * src)
        ref = PC.at[kk, src, p, br, rows]
        return rcopy(ref, ref, h5.at[2 * i + src, 0], h5.at[2 * i + src, 1], other)

    def y0_parts(j):
        p, qt = j // 4, lax.rem(j, 4)
        s = 1 - 2 * p
        yy = m4(s * y)
        ref = PR.at[p, 0, pl.ds(qt * 64, 64)]
        fwd = rcopy(ref, ref, y0s.at[j, 0], y0r.at[j], dev(z, x, m4(y + s), k))
        back = rcopy(ref, ref, y0s.at[j, 1], y0r.at[j], dev(z, x, m4(y - s), k))
        return yy, fwd, back

    def d_parts(j):
        d, qt = j // 4, lax.rem(j, 4)
        rows = pl.ds(qt * 64, 64)
        ref = DG.at[d, rows]
        src_x = jnp.minimum(d, 1)
        s1 = 1 - 2 * lax.rem(d, 2)
        parts = tree(
            0, src_x, 1, s1, s1, lambda e, to: rcopy(ref, ref, ds.at[j, e], dr.at[j], to)
        )
        return parts, d, rows

    @pl.when(k == 0)
    def _():
        @pl.when(y == 0)
        def _():
            h0_copy.start()
            PR[0, 0] = pan[0]

        def y0_step(j, carry):
            yy, fwd, back = y0_parts(j)

            @pl.when(yy != 0)
            def _():
                fwd.wait_recv()

            @pl.when(jnp.logical_and(yy == 0, j == 4))
            def _():
                h1_copy.wait_recv()

            @pl.when(yy <= 1)
            def _():
                fwd.start()

            @pl.when(yy == 0)
            def _():
                back.start()

            p = j // 4

            @pl.when(jnp.logical_or(r == 1, jnp.logical_and(r == 0, p == 0)))
            def _():
                dj = j + 4 * jnp.minimum(r, 1)
                (is_src, conds, copies), d, rows = d_parts(dj)
                DG[d, rows, :] = PR[p, 0, rows, :]
                for cp in copies:
                    cp.start()

            return carry

        lax.fori_loop(0, 8, y0_step, 0)
        for p in range(2):
            h2_copy[p].start()

        def d_step(j, carry):
            (is_src, conds, copies), d, rows = d_parts(j)

            @pl.when(jnp.logical_not(is_src))
            def _():
                copies[0].wait_recv()
                for cond, cp in zip(conds, copies):
                    @pl.when(cond)
                    def _(cp=cp):
                        cp.start()

            return carry

        lax.fori_loop(0, 12, d_step, 0)
        pack()
        start_children()

        AW[0:256, 0:256] = (DG[0] + DG[0].T) * 0.5
        AW[0:256, 256:512] = DG[1].T
        AW[256:512, 0:256] = jnp.zeros((256, 256), F32)
        AW[256:512, 256:512] = (DG[2] + DG[2].T) * 0.5
        factor(AW)
        h3_copy.start()

        def h4_wait(j, carry):
            h4_copy(j).wait_recv()
            return carry

        lax.fori_loop(0, 6, h4_wait, 0)

        def h5_wait(q, carry):
            h5_copy(q // 2, lax.rem(q, 2)).wait_recv()
            return carry

        lax.fori_loop(0, 16 * NH, h5_wait, 0)

    def y1_parts(i, p):
        br = 1 + i // YH
        rows = pl.ds(lax.rem(i, YH) * (256 // YH), 256 // YH)
        s = 1 - 2 * p
        yy = m4(s * y)
        ref = PR.at[p, br, rows]
        j = 2 * i + p
        return yy, br, rcopy(ref, ref, y1s.at[j], y1r.at[j], dev(z, x, m4(y + s), k))

    def xz_place(s):
        row = 2 * y + lax.rem(s, 2) + 8 * (s // 2)
        return row // 4, lax.rem(row, 4)

    def xz_parts(i, s):
        kk, src, p, br, rows = xz_index(i, s)
        ref = PC.at[kk, src, p, br, rows]
        xfirst = lax.rem(i, 2)
        s1 = 1 - 2 * lax.rem(i // 2, 2)
        s2 = 1 - 2 * lax.rem(i // 4, 2)
        q = 4 * i + s
        sz, sx = xz_place(s)
        return tree(
            sz, sx, xfirst, s1, s2, lambda e, to: rcopy(ref, ref, xs_.at[q, e], xr_.at[q], to)
        )

    def depth(s):
        sz, sx = xz_place(s)
        oz, ox = m4(z - sz), m4(x - sx)
        return jnp.minimum(oz, 4 - oz) + jnp.minimum(ox, 4 - ox)

    @pl.when(k == 1)
    def _():
        @pl.when(y == 0)
        def _():
            PR[1, 1:4] = pan[1:4]
            h1_copy.start()
            h0_copy.wait_recv()

        def xz_source(p, br):
            @pl.when(lax.rem(r, 8) // 2 == y)
            def _():
                kk, src = lax.rem(r, 2), r // 8
                PC[kk, src, p, br] = PR[p, br]
                for h in range(NH):
                    i = (p + 2 * lax.rem(br + 3, 4)) * NH + h
                    is_src, conds, copies = xz_parts(i, src * 2 + kk)
                    for cp in copies:
                        cp.start()

                    @pl.when(kk == 0)
                    def _(i=i):
                        h5_copy(i, src).start()

        def y1_step(q, carry):
            p = lax.rem(q, 2)
            yy = m4((1 - 2 * p) * y)
            i = q // 2 - jnp.maximum(yy - 1, 0)

            @pl.when(jnp.logical_and(i >= 0, i < 3 * YH))
            def _():
                _, br, fwd = y1_parts(i, p)

                @pl.when(yy != 0)
                def _():
                    fwd.wait_recv()

                @pl.when(yy < 3)
                def _():
                    fwd.start()

                @pl.when(lax.rem(i, YH) == YH - 1)
                def _():
                    h4_copy(p + 2 * (br - 1)).start()
                    xz_source(p, br)

            return carry

        lax.fori_loop(0, 2 * (3 * YH + 2), y1_step, 0)
        for p in range(2):
            h2_copy[p].wait_recv()
            xz_source(p, 0)
        pack()
        start_children()

        def xz_step(q, carry):
            s = lax.rem(q, 4)
            dep = depth(s)
            i = q // 4 - (dep - 1)

            @pl.when(jnp.logical_and(dep > 0, jnp.logical_and(i >= 0, i < 8 * NH)))
            def _():
                is_src, conds, copies = xz_parts(i, s)
                copies[0].wait_recv()
                for cond, cp in zip(conds, copies):
                    @pl.when(cond)
                    def _(cp=cp):
                        cp.start()

                @pl.when(lax.rem(s, 2) == 0)
                def _():
                    h5_copy(i, s // 2).start()

            return carry

        lax.fori_loop(0, 4 * (8 * NH + 3), xz_step, 0)
        h3_copy.wait_recv()

    i0 = lax.broadcasted_iota(jnp.int32, (256, 256), 0)
    i1 = lax.broadcasted_iota(jnp.int32, (256, 256), 1)
    low = i1 <= i0
    Wh[0], Wl[0] = split(jnp.where(low, AW[0:256, 0:256], 0.0))
    Wh[1], Wl[1] = split(AW[256:512, 0:256])
    Wh[2], Wl[2] = split(jnp.where(low, AW[256:512, 256:512], 0.0))

    def times_w(h, l, w):
        return bdot(h, Wh[w], NT) + (bdot(h, Wl[w], NT) + bdot(l, Wh[w], NT))

    def solve(m0, m1, put):
        h0_, l0_ = split(m0)
        h1_, l1_ = split(m1)
        a = times_w(h0_, l0_, 0)
        put(0, *split(a))
        e = times_w(h0_, l0_, 1) + times_w(h1_, l1_, 2)
        put(1, *split(e))

    def row_solve(i, carry):
        def put(p, hi, lo):
            oh[i, :, pl.ds(p * 256, 256)] = hi
            ol[i, :, pl.ds(p * 256, 256)] = lo

        solve(PR[0, i], PR[1, i], put)
        return carry

    lax.fori_loop(0, 4, row_solve, 0)

    def col_solve(i, carry):
        def put(p, hi, lo):
            oh[4 + i, :, pl.ds(p * 256, 256)] = hi
            ol[4 + i, :, pl.ds(p * 256, 256)] = lo

        solve(PC[k, lax.rem(i, 2), 0, i // 2], PC[k, lax.rem(i, 2), 1, i // 2], put)
        return carry

    lax.fori_loop(0, 8, col_solve, 0)
    outs = [
        pltpu.make_async_copy(oh.at[pl.ds(0, 4)], lrh, osem.at[0]),
        pltpu.make_async_copy(ol.at[pl.ds(0, 4)], lrl, osem.at[1]),
        pltpu.make_async_copy(oh.at[pl.ds(4, 8)], lch, osem.at[2]),
        pltpu.make_async_copy(ol.at[pl.ds(4, 8)], lcl, osem.at[3]),
    ]
    for cp in outs:
        cp.start()

    corner[...] = jnp.zeros((256, 256), F32)

    def diag_block(o):
        t = AW[o : o + 256, o : o + 256].T
        return jnp.where(i1 < i0, t, jnp.where(i1 == i0, 1.0 / t, 0.0))

    @pl.when(jnp.logical_and(r == 0, c == 0))
    def _():
        corner[...] = diag_block(0)

    @pl.when(jnp.logical_and(r == 1, c == 0))
    def _():
        corner[...] = AW[0:256, 256:512].T

    @pl.when(jnp.logical_and(r == 1, c == 1))
    def _():
        corner[...] = diag_block(256)

    @pl.when(k == 0)
    def _():
        @pl.when(y == 0)
        def _():
            h0_copy.wait_send()

        def y0_end(j, carry):
            yy, fwd, back = y0_parts(j)

            @pl.when(yy <= 1)
            def _():
                fwd.wait_send()

            @pl.when(yy == 0)
            def _():
                back.wait_send()

            return carry

        lax.fori_loop(0, 8, y0_end, 0)
        for p in range(2):
            h2_copy[p].wait_send()

        def d_end(j, carry):
            (is_src, conds, copies), d, rows = d_parts(j)
            for cond, cp in zip(conds, copies):
                @pl.when(cond)
                def _(cp=cp):
                    cp.wait_send()

            return carry

        lax.fori_loop(0, 12, d_end, 0)
        h3_copy.wait_send()

    @pl.when(k == 1)
    def _():
        @pl.when(y == 0)
        def _():
            h1_copy.wait_send()

        def y1_end(q, carry):
            yy, br, fwd = y1_parts(q // 2, lax.rem(q, 2))

            @pl.when(yy < 3)
            def _():
                fwd.wait_send()

            return carry

        lax.fori_loop(0, 6 * YH, y1_end, 0)

        def h4_end(j, carry):
            h4_copy(j).wait_send()
            return carry

        lax.fori_loop(0, 6, h4_end, 0)

        def xz_end(q, carry):
            is_src, conds, copies = xz_parts(q // 4, lax.rem(q, 4))
            for cond, cp in zip(conds, copies):
                @pl.when(cond)
                def _(cp=cp):
                    cp.wait_send()

            return carry

        lax.fori_loop(0, 32 * NH, xz_end, 0)

        def h5_end(q, carry):
            h5_copy(q // 2, lax.rem(q, 2)).wait_send()
            return carry

        lax.fori_loop(0, 16 * NH, h5_end, 0)

    wait_children()
    for cp in outs:
        cp.wait()


def exchange(pan, child_blocks, child_rows, child_cols, child_count):
    vm = pl.BlockSpec(memory_space=pltpu.VMEM)
    sm = pl.BlockSpec(memory_space=pltpu.SMEM)
    hbm = pl.BlockSpec(memory_space=pl.ANY)
    dma = pltpu.SemaphoreType.DMA
    return pl.pallas_call(
        comm_kernel,
        out_shape=(
            jax.ShapeDtypeStruct((16, 264, 256), F32),
            jax.ShapeDtypeStruct((4, 256, 512), BF),
            jax.ShapeDtypeStruct((4, 256, 512), BF),
            jax.ShapeDtypeStruct((8, 256, 512), BF),
            jax.ShapeDtypeStruct((8, 256, 512), BF),
            jax.ShapeDtypeStruct((256, 256), F32),
        ),
        in_specs=[vm, vm, vm, vm, sm, sm, sm],
        out_specs=(hbm, hbm, hbm, hbm, hbm, vm),
        scratch_shapes=[
            pltpu.VMEM((16, 264, 256), F32),
            pltpu.VMEM((2, 4, 256, 256), F32),
            pltpu.VMEM((2, 2, 2, 4, 256, 256), F32),
            pltpu.VMEM((3, 256, 256), F32),
            pltpu.VMEM((512, 512), F32),
            pltpu.VMEM((3, 256, 256), BF),
            pltpu.VMEM((3, 256, 256), BF),
            pltpu.VMEM((12, 256, 512), BF),
            pltpu.VMEM((12, 256, 512), BF),
            dma((2,)), dma((2,)), dma((2, 2)), dma((2,)), dma((6, 2)), dma((16 * NH, 2)),
            dma((8, 2)), dma((8,)), dma((6 * YH,)), dma((6 * YH,)),
            dma((12, 4)), dma((12,)), dma, dma((32 * NH, 4)), dma((32 * NH,)),
            dma((8,)), dma((8,)), dma((4,)),
        ],
        compiler_params=pltpu.CompilerParams(
            collective_id=1, has_side_effects=True, vmem_limit_bytes=52 << 20
        ),
        name="exchange",
    )(pan, child_blocks, child_rows, child_cols, child_rows, child_cols, child_count)


def finish(mode, front_ref, recv_ref, lrh_ref, lrl_ref, lch_ref, lcl_ref, corner_ref, out_ref, add_ref, code_ref):
    i=pl.program_id(0)
    r=lax.axis_index("row") if "nomesh" not in mode else 3
    c=lax.axis_index("col") if "nomesh" not in mode else 3
    @pl.when(i==0)
    def _():
        for s in range(16):
            code_ref[s]=jnp.max(recv_ref[s,258:259,:]).astype(jnp.int32)
    add_ref[...]=jnp.zeros_like(add_ref)
    if "noch" not in mode:
        def slot(s,carry):
            code=code_ref[s]
            @pl.when((code>>3)==i)
            def _():
                rows=recv_ref[s,256:257,:].astype(jnp.int32)
                cols=recv_ref[s,257:258,:].astype(jnp.int32)
                t=lax.broadcasted_iota(jnp.int32,(256,256),0)
                R=jnp.where(rows==t,1.0,0.0).astype(BF)
                Q=jnp.where(cols==t,1.0,0.0).astype(BF)
                h,l=split(recv_ref[s,0:256,:])
                p=bdot(R,h,NN)+bdot(R,l,NN)
                h,l=split(p)
                j=code&7
                add_ref[j]=add_ref[j]+(bdot(h,Q,NT)+bdot(l,Q,NT))
            return carry
        lax.fori_loop(0,16,slot,0)
    special=jnp.logical_and(i==0,r<2)
    ah=lrh_ref[0]; al=lrl_ref[0]
    for j in range(8):
        bh=lch_ref[j]; bl=lcl_ref[j]
        if "noup" in mode: u=0.0
        else: u=bdot(ah,bh,NT)+(bdot(ah,bl,NT)+bdot(al,bh,NT))
        v=front_ref[0,:,j,:]+add_ref[j]-u
        out_ref[0,:,j,:]=v
    @pl.when(c<2)
    def _():
        @pl.when(c==0)
        def _(): out_ref[0,:,0,:]=ah[:,0:256].astype(F32)+al[:,0:256].astype(F32)
        @pl.when(c==1)
        def _(): out_ref[0,:,0,:]=ah[:,256:512].astype(F32)+al[:,256:512].astype(F32)
    @pl.when(special)
    def _():
        out_ref[0,:,1:8,:]=jnp.zeros((256,7,256),F32)
        out_ref[0,:,0,:]=corner_ref[...]
def kernel_b(mode,front,recv,lrh,lrl,lch,lcl,corner):
    return pl.pallas_call(functools.partial(finish,mode),grid=(4,),
        out_shape=jax.ShapeDtypeStruct((4,256,8,256),F32),
        in_specs=[pl.BlockSpec((1,256,8,256),lambda i:(i,0,0,0)),
                  pl.BlockSpec((16,264,256),lambda i:(0,0,0)),
                  pl.BlockSpec((1,256,512),lambda i:(i,0,0)),pl.BlockSpec((1,256,512),lambda i:(i,0,0)),
                  pl.BlockSpec((8,256,512),lambda i:(0,0,0)),pl.BlockSpec((8,256,512),lambda i:(0,0,0)),
                  pl.BlockSpec((256,256),lambda i:(0,0))],
        out_specs=pl.BlockSpec((1,256,8,256),lambda i:(i,0,0,0)),
        scratch_shapes=[pltpu.VMEM((8,256,256),F32),pltpu.SMEM((16,),jnp.int32)],
        compiler_params=pltpu.CompilerParams(vmem_limit_bytes=48<<20),name="finish_"+mode.replace(" ","_"))(front,recv,lrh,lrl,lch,lcl,corner)


def local(front, child_blocks, child_rows, child_cols, child_count):
    pan = front[:, :, 0, :]
    recv, lrh, lrl, lch, lcl, corner = exchange(pan, child_blocks, child_rows, child_cols, child_count)
    return kernel_b("", front, recv, lrh, lrl, lch, lcl, corner)


def solution(mesh):
    placed = (
        P(None, "row", None, "col"),
        P(("row", "col"), None, None),
        P(("row", "col"), None),
        P(("row", "col"), None),
        P(("row", "col")),
    )
    return jax.shard_map(
        local, mesh=mesh, in_specs=placed, out_specs=P(None, "row", None, "col"), check_vma=False
    )
```

```python
import functools

import jax
import jax.numpy as jnp
from jax import lax
from jax.experimental import pallas as pl
from jax.experimental.pallas import tpu as pltpu
from jax.sharding import PartitionSpec as P

F32 = jnp.float32
BF = jnp.bfloat16
MESH = pl.DeviceIdType.MESH
TN = (((0,), (0,)), ((), ()))
NT = (((1,), (1,)), ((), ()))
NN = (((1,), (0,)), ((), ()))


def hdot(a, b, dn):
    return lax.dot_general(a, b, dn, precision=lax.Precision.HIGHEST, preferred_element_type=F32)


def bdot(a, b, dn):
    return lax.dot_general(a, b, dn, preferred_element_type=F32)


def split(x):
    hi = x.astype(BF)
    return hi, (x - hi.astype(F32)).astype(BF)


def factor(A, group=8, strip=32):
    ns = 128//strip
    lane = lax.broadcasted_iota(jnp.int32,(strip,128),1)
    sub = lax.broadcasted_iota(jnp.int32,(strip,128),0)
    def tile(J,carry):
        c0 = pl.multiple_of(J*128,128)
        for t in range(ns):
            r0 = pl.multiple_of(c0+strip*t,strip)
            S = [A[pl.ds(r0,strip),128*i:128*i+128] for i in range(4)]
            T = A[pl.ds(r0,strip),pl.ds(c0,128)]
            for s0 in range(0,strip,group):
                cols=[jnp.broadcast_to(T[:,strip*t+s0+a:strip*t+s0+a+1],(strip,128)) for a in range(group)]
                fs=[]
                for a in range(group):
                    s=s0+a
                    rd=1.0/cols[a][s:s+1,:]
                    f=jnp.where(sub>s,cols[a]*rd,0.0)
                    fs.append(f)
                    for b in range(a+1,group):
                        cols[b]=cols[b]-f*cols[b][s:s+1,:]
                for a in range(group):
                    s=s0+a; k=strip*t+s
                    f=fs[a]
                    rowT=jnp.where(lane[:1]==k,1.0,T[s:s+1,:])
                    T=jnp.where((lane==k)&(sub>s),0.0,T)-f*rowT
                    S=[x-f*x[s:s+1,:] for x in S]
            dg=(lane==sub+strip*t)
            d=jnp.sum(jnp.where(dg,T,0.0),axis=1,keepdims=True)
            rs=lax.rsqrt(d)
            rs=rs*(1.5-0.5*d*rs*rs)
            rs=jnp.broadcast_to(rs,(strip,128))
            T=jnp.where(dg,1.0,T)*rs
            for i in range(4): A[pl.ds(r0,strip),128*i:128*i+128]=S[i]*rs
            if t<ns-1:
                n=128-strip*(t+1)
                A[pl.ds(r0,strip),pl.ds(c0,128)]=jnp.where((lane>sub+strip*t)&(lane<strip*(t+1)),0.0,T)
                R=A[pl.ds(r0,strip),:]
                lm=jnp.where(lane>=strip*(t+1),T,0.0)
                upd=hdot(lm,R,TN)
                rb=pl.multiple_of(r0+strip,strip)
                lane_n=lax.broadcasted_iota(jnp.int32,(n,128),1)
                Tt=A[pl.ds(rb,n),pl.ds(c0,128)]
                A[pl.ds(rb,n),pl.ds(c0,128)]=jnp.where((lane_n>=strip*t)&(lane_n<strip*(t+1)),0.0,Tt)
                A[pl.ds(rb,n),:]=A[pl.ds(rb,n),:]-upd[strip*(t+1):]
            A[pl.ds(r0,strip),pl.ds(c0,128)]=T
        R=A[pl.ds(c0,128),:]
        D=A[pl.ds(c0,128),pl.ds(c0,128)]
        i1=lax.broadcasted_iota(jnp.int32,(128,128),1); i0=lax.broadcasted_iota(jnp.int32,(128,128),0)
        D=jnp.where(i1>i0,0.0,D)
        for m in range(1,4):
            @pl.when(m>J)
            def _(m=m):
                lm=A[pl.ds(c0,128),m*128:(m+1)*128]
                A[m*128:(m+1)*128,:]=A[m*128:(m+1)*128,:]-hdot(lm,R,TN)
                A[m*128:(m+1)*128,pl.ds(c0,128)]=-hdot(lm,D,TN)
        return carry
    lax.fori_loop(0,4,tile,0)


DQ = 2
YH = 4
CSTEP = 4
LAG = 1
NH = 1


def m4(v):
    return lax.rem(v + 8, 4)


def comm_kernel(
    pan, cb, crow, ccol, crow_s, ccol_s, cnt_s,
    recv, lrh, lrl, lch, lcl, corner,
    stage, PR, PC, DG, AW, Wh, Wl, oh, ol,
    h1, h3, h4, h5, y0s, y0r, y1s, y1r, ds, dr, dloc, xs_, xr_, cs, cr, osem,
):
    r = lax.axis_index("row")
    c = lax.axis_index("col")
    z, x = r // 4, lax.rem(r, 4)
    y, k = c // 2, lax.rem(c, 2)
    zp, zm = jnp.where(z == 3, 0, z + 1), jnp.where(z == 0, 3, z - 1)
    xp, xm = jnp.where(x == 3, 0, x + 1), jnp.where(x == 0, 3, x - 1)
    yp, ym = jnp.where(y == 3, 0, y + 1), jnp.where(y == 0, 3, y - 1)

    def dev(z, x, y, k):
        return (z * 4 + x, y * 2 + k)

    other = dev(z, x, y, 1 - k)
    b = pltpu.get_barrier_semaphore()
    for d in range(1, 8):
        pl.semaphore_signal(b, inc=1, device_id=(r, lax.rem(c + d, 8)), device_id_type=MESH)
    for s in (1, 3):
        pl.semaphore_signal(b, inc=1, device_id=dev(z, m4(x + s), y, k), device_id_type=MESH)
        pl.semaphore_signal(b, inc=1, device_id=dev(m4(z + s), x, y, k), device_id_type=MESH)
    pl.semaphore_wait(b, 11)

    def rcopy(src, dst, ss, rs, to):
        return pltpu.make_async_remote_copy(
            src_ref=src, dst_ref=dst, send_sem=ss, recv_sem=rs, device_id=to, device_id_type=MESH
        )

    def pack():
        owner = [lax.rem(ccol_s[s, 0] // 256, 8) for s in range(8)]
        live = [(s < cnt_s[0]).astype(jnp.int32) for s in range(8)]
        rank = []
        for s in range(8):
            n = jnp.int32(0)
            for q in range(s):
                n = n + live[q] * (owner[q] == owner[s]).astype(jnp.int32)
            rank.append(n)

        def slot(t, carry):
            idx = jnp.int32(0)
            ok = jnp.int32(0)
            for s in range(8):
                hit = live[s] * (owner[s] * 2 + rank[s] == t).astype(jnp.int32)
                idx = idx + hit * s
                ok = ok + hit
            rows = crow[pl.ds(idx, 1), :]
            cols = ccol[pl.ds(idx, 1), :]
            brow = rows // 4096
            bcol = cols // 2048
            code = jnp.where(ok > 0, brow * 8 + bcol, -1)
            stage[t, 0:256, :] = cb[idx]
            stage[t, 256:257, :] = lax.rem(rows, 256).astype(F32)
            stage[t, 257:258, :] = lax.rem(cols, 256).astype(F32)
            stage[t, 258:259, :] = code.astype(F32)
            stage[t, 259:264, :] = jnp.zeros((5, 256), F32)
            return carry

        lax.fori_loop(0, 16, slot, 0)

    def child_copy(d):
        to = lax.rem(c + d, 8)
        return rcopy(
            stage.at[pl.ds(to * 2, 2)], recv.at[pl.ds(c * 2, 2)], cs.at[d], cr.at[d], (r, to)
        )

    own_copy = pltpu.make_async_copy(stage.at[pl.ds(c * 2, 2)], recv.at[pl.ds(c * 2, 2)], cs.at[0])

    def start_children():
        own_copy.start()
        for d in (1, 7, 2, 6, 3, 5, 4):
            child_copy(d).start()

    def wait_children():
        own_copy.wait()
        for d in range(1, 8):
            child_copy(d).wait()

    def both(v):
        f = lax.rem(v + 4, 4)
        return f, jnp.where(f == 0, 0, 4 - f)

    def tree(oz, ox, xfirst, back1, back2, make):
        def pick(flag, a, b):
            if isinstance(flag, bool):
                return a if flag else b
            return jnp.where(flag, a, b)

        a = pick(xfirst, pick(back1, ox[1], ox[0]), pick(back1, oz[1], oz[0]))
        bb = pick(xfirst, pick(back2, oz[1], oz[0]), pick(back2, ox[1], ox[0]))
        row = z * 4 + x
        z_up, z_dn, x_up, x_dn = zp * 4 + x, zm * 4 + x, z * 4 + xp, z * 4 + xm
        up1, dn1 = pick(xfirst, x_up, z_up), pick(xfirst, x_dn, z_dn)
        up2, dn2 = pick(xfirst, z_up, x_up), pick(xfirst, z_dn, x_dn)
        is_src = a + bb == 0
        conds = (
            jnp.logical_and(bb == 0, a <= 1),
            is_src,
            bb <= 1,
            bb == 0,
        )
        targets = (
            (pick(back1, dn1, up1), c), (pick(back1, up1, dn1), c),
            (pick(back2, dn2, up2), c), (pick(back2, up2, dn2), c),
        )
        copies = [make(e, to) for e, to in enumerate(targets)]
        return is_src, conds, copies

    h1_copies = [
        rcopy(pan.at[i], PR.at[2 * i + 1], h1.at[i, 0], h1.at[i, 1], other) for i in range(4)
    ]
    h3_copy = rcopy(AW, AW, h3.at[0], h3.at[1], other)

    def h4_copy(j):
        return rcopy(PR.at[j], PR.at[j], h4.at[j, 0], h4.at[j, 1], other)

    y_depth = (y, jnp.where(y == 0, 0, 4 - y))
    y_next = (dev(z, x, yp, k), dev(z, x, ym, k))

    def y1_part(br, p, h):
        rows = pl.ds(h * (256 // YH), 256 // YH)
        ref = PR.at[2 * br + p, rows]
        j = (2 * br + p) * YH + h
        return rcopy(ref, ref, y1s.at[j], y1r.at[j], y_next[p])

    def h5_copy(i, src, h):
        ref = PC.at[2 * src, i, pl.ds(h * (256 // NH), 256 // NH)]
        j = (2 * i + src) * NH + h
        return rcopy(ref, ref, h5.at[j, 0], h5.at[j, 1], other)

    def y0_parts(j):
        p, qt = j // DQ, j % DQ
        ref = PR.at[p, pl.ds(qt * (256 // DQ), 256 // DQ)]
        fwd = rcopy(ref, ref, y0s.at[j, 0], y0r.at[j], y_next[p])
        back = rcopy(ref, ref, y0s.at[j, 1], y0r.at[j], y_next[1 - p])
        return p, y_depth[p], fwd, back

    dz_ = both(z)
    dx_ = (both(x), both(x - 1))

    def d_parts(j):
        d, qt = j // DQ, j % DQ
        rows = pl.ds(qt * (256 // DQ), 256 // DQ)
        ref = DG.at[d, rows]
        back = d % 2 == 1
        parts = tree(
            dz_, dx_[min(d, 1)], True, back, back,
            lambda e, to: rcopy(ref, ref, ds.at[j, e], dr.at[j], to),
        )
        return parts, d, rows

    def d_sources(p, qt):
        for row in (0, 1) if p == 0 else (1,):
            @pl.when(r == row)
            def _(row=row):
                d = row + p
                (is_src, conds, copies), d, rows = d_parts(d * DQ + qt)
                DG[d, rows, :] = PR[p, rows, :]
                for cp in copies:
                    cp.start()

    @pl.when(k == 0)
    def _():
        @pl.when(y == 0)
        def _():
            for i in range(4):
                PR[2 * i] = pan[i]
            for cp in h1_copies:
                cp.wait_recv()

        for j in range(2 * DQ):
            p, yy, fwd, back = y0_parts(j)

            @pl.when(yy != 0)
            def _():
                fwd.wait_recv()

            @pl.when(yy <= 1)
            def _():
                fwd.start()

            @pl.when(yy == 0)
            def _():
                back.start()

            if j % DQ == DQ - 1:
                h4_copy(p).start()
            d_sources(p, j % DQ)

        def y1_step(t, carry):
            for h in range(YH):
                for p in range(2):
                    yy = y_depth[p]
                    br = t - yy

                    @pl.when(jnp.logical_and(br >= 1, br <= 3))
                    def _(p=p, yy=yy, br=br, h=h):
                        fwd = y1_part(br, p, h)

                        @pl.when(yy != 0)
                        def _():
                            fwd.wait_recv()

                        @pl.when(yy < 3)
                        def _():
                            fwd.start()

                        if h == YH - 1:
                            h4_copy(2 * br + p).start()

            return carry

        lax.fori_loop(1, 7, y1_step, 0)

        for j in range(3 * DQ):
            (is_src, conds, copies), d, rows = d_parts(j)

            @pl.when(jnp.logical_not(is_src))
            def _():
                copies[0].wait_recv()
                for cond, cp in zip(conds, copies):
                    @pl.when(cond)
                    def _(cp=cp):
                        cp.start()

        pack()
        start_children()

        AW[0:256, 0:256] = (DG[0] + DG[0].T) * 0.5
        AW[0:256, 256:512] = DG[1].T
        AW[256:512, 0:256] = jnp.zeros((256, 256), F32)
        AW[256:512, 256:512] = (DG[2] + DG[2].T) * 0.5
        factor(AW)
        h3_copy.start()

        def h5_wait(i, carry):
            for src in range(2):
                for h in range(NH):
                    h5_copy(i, src, h).wait_recv()
            return carry

        lax.fori_loop(0, 8, h5_wait, 0)

    xz_off = []
    xz_depth = []
    for s in range(4):
        row = 2 * y + s % 2 + 8 * (s // 2)
        oz, ox = both(z - row // 4), both(x - lax.rem(row, 4))
        xz_off.append((oz, ox))
        xz_depth.append(jnp.minimum(oz[0], oz[1]) + jnp.minimum(ox[0], ox[1]))

    def xz_parts(i, s, h):
        ref = PC.at[s, i, pl.ds(h * (256 // NH), 256 // NH)]
        zfirst = jnp.logical_or(i == 3, i == 7)
        back1 = i >= 4
        back2 = jnp.logical_or(jnp.logical_or(i == 1, i == 3), jnp.logical_or(i == 4, i == 6))
        q = (4 * i + s) * NH + h
        oz, ox = xz_off[s]
        return tree(
            oz, ox, jnp.logical_not(zfirst), back1, back2,
            lambda e, to: rcopy(ref, ref, xs_.at[q, e], xr_.at[q], to),
        )

    @pl.when(k == 1)
    def _():
        @pl.when(y == 0)
        def _():
            for cp in h1_copies:
                cp.start()

        pack()

        def xz_step(t, carry):
            for h in range(NH):
                for s in range(4):
                    dep = xz_depth[s]
                    i = t - LAG * dep

                    @pl.when(jnp.logical_and(i >= 0, i < 8))
                    def _(s=s, dep=dep, i=i, h=h):
                        _, conds, copies = xz_parts(i, s, h)

                        @pl.when(dep == 0)
                        def _():
                            if h == 0:
                                h4_copy(i).wait_recv()
                                PC[s, i] = PR[i]

                        @pl.when(dep != 0)
                        def _():
                            copies[0].wait_recv()

                        for cond, cp in zip(conds, copies):
                            @pl.when(cond)
                            def _(cp=cp):
                                cp.start()

                        if s % 2 == 0:
                            h5_copy(i, s // 2, h).start()

            return carry

        lax.fori_loop(0, CSTEP, xz_step, 0)
        start_children()
        lax.fori_loop(CSTEP, 8 + 4 * LAG, xz_step, 0)

        def h4_wait(j, carry):
            h4_copy(j).wait_recv()
            return carry

        @pl.when(lax.rem(r, 8) // 2 != y)
        def _():
            lax.fori_loop(0, 8, h4_wait, 0)

        h3_copy.wait_recv()

    i0 = lax.broadcasted_iota(jnp.int32, (256, 256), 0)
    i1 = lax.broadcasted_iota(jnp.int32, (256, 256), 1)
    low = i1 <= i0
    Wh[0], Wl[0] = split(jnp.where(low, AW[0:256, 0:256], 0.0))
    Wh[1], Wl[1] = split(AW[256:512, 0:256])
    Wh[2], Wl[2] = split(jnp.where(low, AW[256:512, 256:512], 0.0))

    def times_w(h, l, w):
        return bdot(h, Wh[w], NT) + (bdot(h, Wl[w], NT) + bdot(l, Wh[w], NT))

    def solve(m0, m1, put):
        h0_, l0_ = split(m0)
        h1_, l1_ = split(m1)
        a = times_w(h0_, l0_, 0)
        put(0, *split(a))
        e = times_w(h0_, l0_, 1) + times_w(h1_, l1_, 2)
        put(1, *split(e))

    def row_solve(i, carry):
        def put(p, hi, lo):
            oh[i, :, pl.ds(p * 256, 256)] = hi
            ol[i, :, pl.ds(p * 256, 256)] = lo

        solve(PR[2 * i], PR[2 * i + 1], put)
        return carry

    lax.fori_loop(0, 4, row_solve, 0)

    def col_solve(i, carry):
        def put(p, hi, lo):
            oh[4 + i, :, pl.ds(p * 256, 256)] = hi
            ol[4 + i, :, pl.ds(p * 256, 256)] = lo

        row_set, j = k + 2 * lax.rem(i, 2), 2 * (i // 2)
        solve(PC[row_set, j], PC[row_set, j + 1], put)
        return carry

    lax.fori_loop(0, 8, col_solve, 0)
    outs = [
        pltpu.make_async_copy(oh.at[pl.ds(0, 4)], lrh, osem.at[0]),
        pltpu.make_async_copy(ol.at[pl.ds(0, 4)], lrl, osem.at[1]),
        pltpu.make_async_copy(oh.at[pl.ds(4, 8)], lch, osem.at[2]),
        pltpu.make_async_copy(ol.at[pl.ds(4, 8)], lcl, osem.at[3]),
    ]
    for cp in outs:
        cp.start()

    corner[...] = jnp.zeros((256, 256), F32)

    def diag_block(o):
        t = AW[o : o + 256, o : o + 256].T
        return jnp.where(i1 < i0, t, jnp.where(i1 == i0, 1.0 / t, 0.0))

    @pl.when(jnp.logical_and(r == 0, c == 0))
    def _():
        corner[...] = diag_block(0)

    @pl.when(jnp.logical_and(r == 1, c == 0))
    def _():
        corner[...] = AW[0:256, 256:512].T

    @pl.when(jnp.logical_and(r == 1, c == 1))
    def _():
        corner[...] = diag_block(256)

    @pl.when(k == 0)
    def _():
        for j in range(2 * DQ):
            p, yy, fwd, back = y0_parts(j)

            @pl.when(yy <= 1)
            def _():
                fwd.wait_send()

            @pl.when(yy == 0)
            def _():
                back.wait_send()

        def y1_end(br, carry):
            for p in range(2):
                @pl.when(y_depth[p] < 3)
                def _(p=p):
                    for h in range(YH):
                        y1_part(br, p, h).wait_send()

            return carry

        lax.fori_loop(1, 4, y1_end, 0)

        def h4_end(j, carry):
            h4_copy(j).wait_send()
            return carry

        lax.fori_loop(0, 8, h4_end, 0)

        for j in range(3 * DQ):
            (is_src, conds, copies), d, rows = d_parts(j)
            for cond, cp in zip(conds, copies):
                @pl.when(cond)
                def _(cp=cp):
                    cp.wait_send()

        h3_copy.wait_send()

    @pl.when(k == 1)
    def _():
        @pl.when(y == 0)
        def _():
            for cp in h1_copies:
                cp.wait_send()

        def xz_end(i, carry):
            for s in range(4):
                for h in range(NH):
                    _, conds, copies = xz_parts(i, s, h)
                    for cond, cp in zip(conds, copies):
                        @pl.when(cond)
                        def _(cp=cp):
                            cp.wait_send()

                    if s % 2 == 0:
                        h5_copy(i, s // 2, h).wait_send()

            return carry

        lax.fori_loop(0, 8, xz_end, 0)

    wait_children()
    for cp in outs:
        cp.wait()


def exchange(pan, child_blocks, child_rows, child_cols, child_count):
    vm = pl.BlockSpec(memory_space=pltpu.VMEM)
    sm = pl.BlockSpec(memory_space=pltpu.SMEM)
    hbm = pl.BlockSpec(memory_space=pl.ANY)
    dma = pltpu.SemaphoreType.DMA
    return pl.pallas_call(
        comm_kernel,
        out_shape=(
            jax.ShapeDtypeStruct((16, 264, 256), F32),
            jax.ShapeDtypeStruct((4, 256, 512), BF),
            jax.ShapeDtypeStruct((4, 256, 512), BF),
            jax.ShapeDtypeStruct((8, 256, 512), BF),
            jax.ShapeDtypeStruct((8, 256, 512), BF),
            jax.ShapeDtypeStruct((256, 256), F32),
        ),
        in_specs=[vm, vm, vm, vm, sm, sm, sm],
        out_specs=(hbm, hbm, hbm, hbm, hbm, vm),
        scratch_shapes=[
            pltpu.VMEM((16, 264, 256), F32),
            pltpu.VMEM((8, 256, 256), F32),
            pltpu.VMEM((4, 8, 256, 256), F32),
            pltpu.VMEM((3, 256, 256), F32),
            pltpu.VMEM((512, 512), F32),
            pltpu.VMEM((3, 256, 256), BF),
            pltpu.VMEM((3, 256, 256), BF),
            pltpu.VMEM((12, 256, 512), BF),
            pltpu.VMEM((12, 256, 512), BF),
            dma((4, 2)), dma((2,)), dma((8, 2)), dma((16 * NH, 2)),
            dma((8, 2)), dma((8,)), dma((8 * YH,)), dma((8 * YH,)),
            dma((12, 4)), dma((12,)), dma, dma((32 * NH, 4)), dma((32 * NH,)),
            dma((8,)), dma((8,)), dma((4,)),
        ],
        compiler_params=pltpu.CompilerParams(
            collective_id=1, has_side_effects=True, vmem_limit_bytes=52 << 20
        ),
        name="exchange",
    )(pan, child_blocks, child_rows, child_cols, child_rows, child_cols, child_count)


def finish(mode, front_ref, recv_ref, lrh_ref, lrl_ref, lch_ref, lcl_ref, corner_ref, out_ref, add_ref, code_ref):
    i=pl.program_id(0)
    r=lax.axis_index("row") if "nomesh" not in mode else 3
    c=lax.axis_index("col") if "nomesh" not in mode else 3
    @pl.when(i==0)
    def _():
        for s in range(16):
            code_ref[s]=jnp.max(recv_ref[s,258:259,:]).astype(jnp.int32)
    add_ref[...]=jnp.zeros_like(add_ref)
    if "noch" not in mode:
        def slot(s,carry):
            code=code_ref[s]
            @pl.when((code>>3)==i)
            def _():
                rows=recv_ref[s,256:257,:].astype(jnp.int32)
                cols=recv_ref[s,257:258,:].astype(jnp.int32)
                t=lax.broadcasted_iota(jnp.int32,(256,256),0)
                R=jnp.where(rows==t,1.0,0.0).astype(BF)
                Q=jnp.where(cols==t,1.0,0.0).astype(BF)
                h,l=split(recv_ref[s,0:256,:])
                p=bdot(R,h,NN)+bdot(R,l,NN)
                h,l=split(p)
                j=code&7
                add_ref[j]=add_ref[j]+(bdot(h,Q,NT)+bdot(l,Q,NT))
            return carry
        lax.fori_loop(0,16,slot,0)
    special=jnp.logical_and(i==0,r<2)
    ah=lrh_ref[0]; al=lrl_ref[0]
    for j in range(8):
        bh=lch_ref[j]; bl=lcl_ref[j]
        if "noup" in mode: u=0.0
        else: u=bdot(ah,bh,NT)+(bdot(ah,bl,NT)+bdot(al,bh,NT))
        v=front_ref[0,:,j,:]+add_ref[j]-u
        out_ref[0,:,j,:]=v
    @pl.when(c<2)
    def _():
        @pl.when(c==0)
        def _(): out_ref[0,:,0,:]=ah[:,0:256].astype(F32)+al[:,0:256].astype(F32)
        @pl.when(c==1)
        def _(): out_ref[0,:,0,:]=ah[:,256:512].astype(F32)+al[:,256:512].astype(F32)
    @pl.when(special)
    def _():
        out_ref[0,:,1:8,:]=jnp.zeros((256,7,256),F32)
        out_ref[0,:,0,:]=corner_ref[...]
def kernel_b(mode,front,recv,lrh,lrl,lch,lcl,corner):
    return pl.pallas_call(functools.partial(finish,mode),grid=(4,),
        out_shape=jax.ShapeDtypeStruct((4,256,8,256),F32),
        in_specs=[pl.BlockSpec((1,256,8,256),lambda i:(i,0,0,0)),
                  pl.BlockSpec((16,264,256),lambda i:(0,0,0)),
                  pl.BlockSpec((1,256,512),lambda i:(i,0,0)),pl.BlockSpec((1,256,512),lambda i:(i,0,0)),
                  pl.BlockSpec((8,256,512),lambda i:(0,0,0)),pl.BlockSpec((8,256,512),lambda i:(0,0,0)),
                  pl.BlockSpec((256,256),lambda i:(0,0))],
        out_specs=pl.BlockSpec((1,256,8,256),lambda i:(i,0,0,0)),
        scratch_shapes=[pltpu.VMEM((8,256,256),F32),pltpu.SMEM((16,),jnp.int32)],
        compiler_params=pltpu.CompilerParams(vmem_limit_bytes=48<<20),name="finish_"+mode.replace(" ","_"))(front,recv,lrh,lrl,lch,lcl,corner)


def local(front, child_blocks, child_rows, child_cols, child_count):
    pan = front[:, :, 0, :]
    recv, lrh, lrl, lch, lcl, corner = exchange(pan, child_blocks, child_rows, child_cols, child_count)
    return kernel_b("", front, recv, lrh, lrl, lch, lcl, corner)


def solution(mesh):
    placed = (
        P(None, "row", None, "col"),
        P(("row", "col"), None, None),
        P(("row", "col"), None),
        P(("row", "col"), None),
        P(("row", "col")),
    )
    return jax.shard_map(
        local, mesh=mesh, in_specs=placed, out_specs=P(None, "row", None, "col"), check_vma=False
    )
```

```python
import functools

import jax
import jax.numpy as jnp
from jax import lax
from jax.experimental import pallas as pl
from jax.experimental.pallas import tpu as pltpu
from jax.sharding import PartitionSpec as P

F32 = jnp.float32
BF = jnp.bfloat16
MESH = pl.DeviceIdType.MESH
TN = (((0,), (0,)), ((), ()))
NT = (((1,), (1,)), ((), ()))
NN = (((1,), (0,)), ((), ()))


def hdot(a, b, dn):
    return lax.dot_general(a, b, dn, precision=lax.Precision.HIGHEST, preferred_element_type=F32)


def bdot(a, b, dn):
    return lax.dot_general(a, b, dn, preferred_element_type=F32)


def split(x):
    hi = x.astype(BF)
    return hi, (x - hi.astype(F32)).astype(BF)


def factor(A, group=8, strip=32):
    ns = 128//strip
    lane = lax.broadcasted_iota(jnp.int32,(strip,128),1)
    sub = lax.broadcasted_iota(jnp.int32,(strip,128),0)
    def tile(J,carry):
        c0 = pl.multiple_of(J*128,128)
        for t in range(ns):
            r0 = pl.multiple_of(c0+strip*t,strip)
            S = [A[pl.ds(r0,strip),128*i:128*i+128] for i in range(4)]
            T = A[pl.ds(r0,strip),pl.ds(c0,128)]
            for s0 in range(0,strip,group):
                cols=[jnp.broadcast_to(T[:,strip*t+s0+a:strip*t+s0+a+1],(strip,128)) for a in range(group)]
                fs=[]
                for a in range(group):
                    s=s0+a
                    rd=1.0/cols[a][s:s+1,:]
                    f=jnp.where(sub>s,cols[a]*rd,0.0)
                    fs.append(f)
                    for b in range(a+1,group):
                        cols[b]=cols[b]-f*cols[b][s:s+1,:]
                for a in range(group):
                    s=s0+a; k=strip*t+s
                    f=fs[a]
                    rowT=jnp.where(lane[:1]==k,1.0,T[s:s+1,:])
                    T=jnp.where((lane==k)&(sub>s),0.0,T)-f*rowT
                    S=[x-f*x[s:s+1,:] for x in S]
            dg=(lane==sub+strip*t)
            d=jnp.sum(jnp.where(dg,T,0.0),axis=1,keepdims=True)
            rs=lax.rsqrt(d)
            rs=rs*(1.5-0.5*d*rs*rs)
            rs=jnp.broadcast_to(rs,(strip,128))
            T=jnp.where(dg,1.0,T)*rs
            for i in range(4): A[pl.ds(r0,strip),128*i:128*i+128]=S[i]*rs
            if t<ns-1:
                n=128-strip*(t+1)
                A[pl.ds(r0,strip),pl.ds(c0,128)]=jnp.where((lane>sub+strip*t)&(lane<strip*(t+1)),0.0,T)
                R=A[pl.ds(r0,strip),:]
                lm=jnp.where(lane>=strip*(t+1),T,0.0)
                upd=hdot(lm,R,TN)
                rb=pl.multiple_of(r0+strip,strip)
                lane_n=lax.broadcasted_iota(jnp.int32,(n,128),1)
                Tt=A[pl.ds(rb,n),pl.ds(c0,128)]
                A[pl.ds(rb,n),pl.ds(c0,128)]=jnp.where((lane_n>=strip*t)&(lane_n<strip*(t+1)),0.0,Tt)
                A[pl.ds(rb,n),:]=A[pl.ds(rb,n),:]-upd[strip*(t+1):]
            A[pl.ds(r0,strip),pl.ds(c0,128)]=T
        R=A[pl.ds(c0,128),:]
        D=A[pl.ds(c0,128),pl.ds(c0,128)]
        i1=lax.broadcasted_iota(jnp.int32,(128,128),1); i0=lax.broadcasted_iota(jnp.int32,(128,128),0)
        D=jnp.where(i1>i0,0.0,D)
        for m in range(1,4):
            @pl.when(m>J)
            def _(m=m):
                lm=A[pl.ds(c0,128),m*128:(m+1)*128]
                A[m*128:(m+1)*128,:]=A[m*128:(m+1)*128,:]-hdot(lm,R,TN)
                A[m*128:(m+1)*128,pl.ds(c0,128)]=-hdot(lm,D,TN)
        return carry
    lax.fori_loop(0,4,tile,0)


DQ = 2
YH = 4
CSTEP = 4
LAG = 1
NH = 1


def m4(v):
    return lax.rem(v + 8, 4)


def comm_kernel(
    front, cb_in, crow, ccol, crow_s, ccol_s, cnt_s,
    recv, lrh, lrl, lch, lcl, corner,
    fbuf, pan, cb, lsem,
    stage, PR, PC, DG, AW, Wh, Wl,
    h1, h3, h4, h5, y0s, y0r, y1s, y1r, ds, dr, dloc, xs_, xr_, cs, cr,
):
    r = lax.axis_index("row")
    c = lax.axis_index("col")
    z, x = r // 4, lax.rem(r, 4)
    y, k = c // 2, lax.rem(c, 2)
    zp, zm = jnp.where(z == 3, 0, z + 1), jnp.where(z == 0, 3, z - 1)
    xp, xm = jnp.where(x == 3, 0, x + 1), jnp.where(x == 0, 3, x - 1)
    yp, ym = jnp.where(y == 3, 0, y + 1), jnp.where(y == 0, 3, y - 1)

    def dev(z, x, y, k):
        return (z * 4 + x, y * 2 + k)

    other = dev(z, x, y, 1 - k)
    front_copies = [
        pltpu.make_async_copy(front.at[i], fbuf.at[i], lsem.at[i]) for i in range(4)
    ]
    cb_copy = pltpu.make_async_copy(cb_in, cb, lsem.at[4])

    @pl.when(y == 0)
    def _():
        for cp in front_copies:
            cp.start()

    cb_copy.start()

    b = pltpu.get_barrier_semaphore()
    for d in range(1, 8):
        pl.semaphore_signal(b, inc=1, device_id=(r, lax.rem(c + d, 8)), device_id_type=MESH)
    for s in (1, 3):
        pl.semaphore_signal(b, inc=1, device_id=dev(z, m4(x + s), y, k), device_id_type=MESH)
        pl.semaphore_signal(b, inc=1, device_id=dev(m4(z + s), x, y, k), device_id_type=MESH)
    pl.semaphore_wait(b, 11)

    def rcopy(src, dst, ss, rs, to):
        return pltpu.make_async_remote_copy(
            src_ref=src, dst_ref=dst, send_sem=ss, recv_sem=rs, device_id=to, device_id_type=MESH
        )

    def pack():
        owner = [lax.rem(ccol_s[s, 0] // 256, 8) for s in range(8)]
        live = [(s < cnt_s[0]).astype(jnp.int32) for s in range(8)]
        rank = []
        for s in range(8):
            n = jnp.int32(0)
            for q in range(s):
                n = n + live[q] * (owner[q] == owner[s]).astype(jnp.int32)
            rank.append(n)

        def slot(t, carry):
            idx = jnp.int32(0)
            ok = jnp.int32(0)
            for s in range(8):
                hit = live[s] * (owner[s] * 2 + rank[s] == t).astype(jnp.int32)
                idx = idx + hit * s
                ok = ok + hit
            rows = crow[pl.ds(idx, 1), :]
            cols = ccol[pl.ds(idx, 1), :]
            brow = rows // 4096
            bcol = cols // 2048
            code = jnp.where(ok > 0, brow * 8 + bcol, -1)
            stage[t, 0:256, :] = cb[idx]
            stage[t, 256:257, :] = lax.rem(rows, 256).astype(F32)
            stage[t, 257:258, :] = lax.rem(cols, 256).astype(F32)
            stage[t, 258:259, :] = code.astype(F32)
            stage[t, 259:264, :] = jnp.zeros((5, 256), F32)
            return carry

        lax.fori_loop(0, 16, slot, 0)

    def child_copy(d):
        to = lax.rem(c + d, 8)
        return rcopy(
            stage.at[pl.ds(to * 2, 2)], recv.at[pl.ds(c * 2, 2)], cs.at[d], cr.at[d], (r, to)
        )

    own_copy = pltpu.make_async_copy(stage.at[pl.ds(c * 2, 2)], recv.at[pl.ds(c * 2, 2)], cs.at[0])

    def start_children():
        own_copy.start()
        for d in (1, 7, 2, 6, 3, 5, 4):
            child_copy(d).start()

    def wait_children():
        own_copy.wait()
        for d in range(1, 8):
            child_copy(d).wait()

    def both(v):
        f = lax.rem(v + 4, 4)
        return f, jnp.where(f == 0, 0, 4 - f)

    def tree(oz, ox, xfirst, back1, back2, make):
        def pick(flag, a, b):
            if isinstance(flag, bool):
                return a if flag else b
            return jnp.where(flag, a, b)

        a = pick(xfirst, pick(back1, ox[1], ox[0]), pick(back1, oz[1], oz[0]))
        bb = pick(xfirst, pick(back2, oz[1], oz[0]), pick(back2, ox[1], ox[0]))
        row = z * 4 + x
        z_up, z_dn, x_up, x_dn = zp * 4 + x, zm * 4 + x, z * 4 + xp, z * 4 + xm
        up1, dn1 = pick(xfirst, x_up, z_up), pick(xfirst, x_dn, z_dn)
        up2, dn2 = pick(xfirst, z_up, x_up), pick(xfirst, z_dn, x_dn)
        is_src = a + bb == 0
        conds = (
            jnp.logical_and(bb == 0, a <= 1),
            is_src,
            bb <= 1,
            bb == 0,
        )
        targets = (
            (pick(back1, dn1, up1), c), (pick(back1, up1, dn1), c),
            (pick(back2, dn2, up2), c), (pick(back2, up2, dn2), c),
        )
        copies = [make(e, to) for e, to in enumerate(targets)]
        return is_src, conds, copies

    h1_copies = [
        rcopy(pan.at[i], PR.at[2 * i + 1], h1.at[i, 0], h1.at[i, 1], other) for i in range(4)
    ]
    h3_copy = rcopy(AW, AW, h3.at[0], h3.at[1], other)

    def h4_copy(j):
        return rcopy(PR.at[j], PR.at[j], h4.at[j, 0], h4.at[j, 1], other)

    y_depth = (y, jnp.where(y == 0, 0, 4 - y))
    y_next = (dev(z, x, yp, k), dev(z, x, ym, k))

    def y1_part(br, p, h):
        rows = pl.ds(h * (256 // YH), 256 // YH)
        ref = PR.at[2 * br + p, rows]
        j = (2 * br + p) * YH + h
        return rcopy(ref, ref, y1s.at[j], y1r.at[j], y_next[p])

    def h5_copy(i, src, h):
        ref = PC.at[2 * src, i, pl.ds(h * (256 // NH), 256 // NH)]
        j = (2 * i + src) * NH + h
        return rcopy(ref, ref, h5.at[j, 0], h5.at[j, 1], other)

    def y0_parts(j):
        p, qt = j // DQ, j % DQ
        ref = PR.at[p, pl.ds(qt * (256 // DQ), 256 // DQ)]
        fwd = rcopy(ref, ref, y0s.at[j, 0], y0r.at[j], y_next[p])
        back = rcopy(ref, ref, y0s.at[j, 1], y0r.at[j], y_next[1 - p])
        return p, y_depth[p], fwd, back

    dz_ = both(z)
    dx_ = (both(x), both(x - 1))

    def d_parts(j):
        d, qt = j // DQ, j % DQ
        rows = pl.ds(qt * (256 // DQ), 256 // DQ)
        ref = DG.at[d, rows]
        back = d % 2 == 1
        parts = tree(
            dz_, dx_[min(d, 1)], True, back, back,
            lambda e, to: rcopy(ref, ref, ds.at[j, e], dr.at[j], to),
        )
        return parts, d, rows

    def d_sources(p, qt):
        for row in (0, 1) if p == 0 else (1,):
            @pl.when(r == row)
            def _(row=row):
                d = row + p
                (is_src, conds, copies), d, rows = d_parts(d * DQ + qt)
                DG[d, rows, :] = PR[p, rows, :]
                for cp in copies:
                    cp.start()

    @pl.when(k == 0)
    def _():
        @pl.when(y == 0)
        def _():
            for i in range(4):
                front_copies[i].wait()
                PR[2 * i] = fbuf[i, :, 0, :]
            for cp in h1_copies:
                cp.wait_recv()

        for j in range(2 * DQ):
            p, yy, fwd, back = y0_parts(j)

            @pl.when(yy != 0)
            def _():
                fwd.wait_recv()

            @pl.when(yy <= 1)
            def _():
                fwd.start()

            @pl.when(yy == 0)
            def _():
                back.start()

            if j % DQ == DQ - 1:
                h4_copy(p).start()
            d_sources(p, j % DQ)

        def y1_step(t, carry):
            for h in range(YH):
                for p in range(2):
                    yy = y_depth[p]
                    br = t - yy

                    @pl.when(jnp.logical_and(br >= 1, br <= 3))
                    def _(p=p, yy=yy, br=br, h=h):
                        fwd = y1_part(br, p, h)

                        @pl.when(yy != 0)
                        def _():
                            fwd.wait_recv()

                        @pl.when(yy < 3)
                        def _():
                            fwd.start()

                        if h == YH - 1:
                            h4_copy(2 * br + p).start()

            return carry

        lax.fori_loop(1, 7, y1_step, 0)

        for j in range(3 * DQ):
            (is_src, conds, copies), d, rows = d_parts(j)

            @pl.when(jnp.logical_not(is_src))
            def _():
                copies[0].wait_recv()
                for cond, cp in zip(conds, copies):
                    @pl.when(cond)
                    def _(cp=cp):
                        cp.start()

        cb_copy.wait()
        pack()
        start_children()

        AW[0:256, 0:256] = (DG[0] + DG[0].T) * 0.5
        AW[0:256, 256:512] = DG[1].T
        AW[256:512, 0:256] = jnp.zeros((256, 256), F32)
        AW[256:512, 256:512] = (DG[2] + DG[2].T) * 0.5
        factor(AW)
        h3_copy.start()

        def h5_wait(i, carry):
            for src in range(2):
                for h in range(NH):
                    h5_copy(i, src, h).wait_recv()
            return carry

        lax.fori_loop(0, 8, h5_wait, 0)

    xz_off = []
    xz_depth = []
    for s in range(4):
        row = 2 * y + s % 2 + 8 * (s // 2)
        oz, ox = both(z - row // 4), both(x - lax.rem(row, 4))
        xz_off.append((oz, ox))
        xz_depth.append(jnp.minimum(oz[0], oz[1]) + jnp.minimum(ox[0], ox[1]))

    def xz_parts(i, s, h):
        ref = PC.at[s, i, pl.ds(h * (256 // NH), 256 // NH)]
        zfirst = jnp.logical_or(i == 3, i == 7)
        back1 = i >= 4
        back2 = jnp.logical_or(jnp.logical_or(i == 1, i == 3), jnp.logical_or(i == 4, i == 6))
        q = (4 * i + s) * NH + h
        oz, ox = xz_off[s]
        return tree(
            oz, ox, jnp.logical_not(zfirst), back1, back2,
            lambda e, to: rcopy(ref, ref, xs_.at[q, e], xr_.at[q], to),
        )

    @pl.when(k == 1)
    def _():
        @pl.when(y == 0)
        def _():
            for i in range(4):
                front_copies[i].wait()
                pan[i] = fbuf[i, :, 0, :]
                h1_copies[i].start()

        cb_copy.wait()
        pack()

        def xz_step(t, carry):
            for h in range(NH):
                for s in range(4):
                    dep = xz_depth[s]
                    i = t - LAG * dep

                    @pl.when(jnp.logical_and(i >= 0, i < 8))
                    def _(s=s, dep=dep, i=i, h=h):
                        _, conds, copies = xz_parts(i, s, h)

                        @pl.when(dep == 0)
                        def _():
                            if h == 0:
                                h4_copy(i).wait_recv()
                                PC[s, i] = PR[i]

                        @pl.when(dep != 0)
                        def _():
                            copies[0].wait_recv()

                        for cond, cp in zip(conds, copies):
                            @pl.when(cond)
                            def _(cp=cp):
                                cp.start()

                        if s % 2 == 0:
                            h5_copy(i, s // 2, h).start()

            return carry

        lax.fori_loop(0, CSTEP, xz_step, 0)
        start_children()
        lax.fori_loop(CSTEP, 8 + 4 * LAG, xz_step, 0)

        def h4_wait(j, carry):
            h4_copy(j).wait_recv()
            return carry

        @pl.when(lax.rem(r, 8) // 2 != y)
        def _():
            lax.fori_loop(0, 8, h4_wait, 0)

        h3_copy.wait_recv()

    i0 = lax.broadcasted_iota(jnp.int32, (256, 256), 0)
    i1 = lax.broadcasted_iota(jnp.int32, (256, 256), 1)
    low = i1 <= i0
    Wh[0], Wl[0] = split(jnp.where(low, AW[0:256, 0:256], 0.0))
    Wh[1], Wl[1] = split(AW[256:512, 0:256])
    Wh[2], Wl[2] = split(jnp.where(low, AW[256:512, 256:512], 0.0))

    def times_w(h, l, w):
        return bdot(h, Wh[w], NT) + (bdot(h, Wl[w], NT) + bdot(l, Wh[w], NT))

    def solve(m0, m1, put):
        h0_, l0_ = split(m0)
        h1_, l1_ = split(m1)
        a = times_w(h0_, l0_, 0)
        put(0, *split(a))
        e = times_w(h0_, l0_, 1) + times_w(h1_, l1_, 2)
        put(1, *split(e))

    def row_solve(i, carry):
        def put(p, hi, lo):
            lrh[i, :, pl.ds(p * 256, 256)] = hi
            lrl[i, :, pl.ds(p * 256, 256)] = lo

        solve(PR[2 * i], PR[2 * i + 1], put)
        return carry

    lax.fori_loop(0, 4, row_solve, 0)

    def col_solve(i, carry):
        def put(p, hi, lo):
            lch[i, :, pl.ds(p * 256, 256)] = hi
            lcl[i, :, pl.ds(p * 256, 256)] = lo

        row_set, j = k + 2 * lax.rem(i, 2), 2 * (i // 2)
        solve(PC[row_set, j], PC[row_set, j + 1], put)
        return carry

    lax.fori_loop(0, 8, col_solve, 0)
    corner[...] = jnp.zeros((256, 256), F32)

    def diag_block(o):
        t = AW[o : o + 256, o : o + 256].T
        return jnp.where(i1 < i0, t, jnp.where(i1 == i0, 1.0 / t, 0.0))

    @pl.when(jnp.logical_and(r == 0, c == 0))
    def _():
        corner[...] = diag_block(0)

    @pl.when(jnp.logical_and(r == 1, c == 0))
    def _():
        corner[...] = AW[0:256, 256:512].T

    @pl.when(jnp.logical_and(r == 1, c == 1))
    def _():
        corner[...] = diag_block(256)

    @pl.when(k == 0)
    def _():
        for j in range(2 * DQ):
            p, yy, fwd, back = y0_parts(j)

            @pl.when(yy <= 1)
            def _():
                fwd.wait_send()

            @pl.when(yy == 0)
            def _():
                back.wait_send()

        def y1_end(br, carry):
            for p in range(2):
                @pl.when(y_depth[p] < 3)
                def _(p=p):
                    for h in range(YH):
                        y1_part(br, p, h).wait_send()

            return carry

        lax.fori_loop(1, 4, y1_end, 0)

        def h4_end(j, carry):
            h4_copy(j).wait_send()
            return carry

        lax.fori_loop(0, 8, h4_end, 0)

        for j in range(3 * DQ):
            (is_src, conds, copies), d, rows = d_parts(j)
            for cond, cp in zip(conds, copies):
                @pl.when(cond)
                def _(cp=cp):
                    cp.wait_send()

        h3_copy.wait_send()

    @pl.when(k == 1)
    def _():
        @pl.when(y == 0)
        def _():
            for cp in h1_copies:
                cp.wait_send()

        def xz_end(i, carry):
            for s in range(4):
                for h in range(NH):
                    _, conds, copies = xz_parts(i, s, h)
                    for cond, cp in zip(conds, copies):
                        @pl.when(cond)
                        def _(cp=cp):
                            cp.wait_send()

                    if s % 2 == 0:
                        h5_copy(i, s // 2, h).wait_send()

            return carry

        lax.fori_loop(0, 8, xz_end, 0)

    wait_children()


def exchange(front, child_blocks, child_rows, child_cols, child_count):
    vm = pl.BlockSpec(memory_space=pltpu.VMEM)
    sm = pl.BlockSpec(memory_space=pltpu.SMEM)
    hbm = pl.BlockSpec(memory_space=pltpu.HBM)
    dma = pltpu.SemaphoreType.DMA
    return pl.pallas_call(
        comm_kernel,
        out_shape=(
            jax.ShapeDtypeStruct((16, 264, 256), F32),
            jax.ShapeDtypeStruct((4, 256, 512), BF),
            jax.ShapeDtypeStruct((4, 256, 512), BF),
            jax.ShapeDtypeStruct((8, 256, 512), BF),
            jax.ShapeDtypeStruct((8, 256, 512), BF),
            jax.ShapeDtypeStruct((256, 256), F32),
        ),
        in_specs=[hbm, hbm, vm, vm, sm, sm, sm],
        out_specs=(vm, vm, vm, vm, vm, vm),
        scratch_shapes=[
            pltpu.VMEM((4, 256, 8, 256), F32),
            pltpu.VMEM((4, 256, 256), F32),
            pltpu.VMEM((8, 256, 256), F32),
            dma((5,)),
            pltpu.VMEM((16, 264, 256), F32),
            pltpu.VMEM((8, 256, 256), F32),
            pltpu.VMEM((4, 8, 256, 256), F32),
            pltpu.VMEM((3, 256, 256), F32),
            pltpu.VMEM((512, 512), F32),
            pltpu.VMEM((3, 256, 256), BF),
            pltpu.VMEM((3, 256, 256), BF),
            dma((4, 2)), dma((2,)), dma((8, 2)), dma((16 * NH, 2)),
            dma((8, 2)), dma((8,)), dma((8 * YH,)), dma((8 * YH,)),
            dma((12, 4)), dma((12,)), dma, dma((32 * NH, 4)), dma((32 * NH,)),
            dma((8,)), dma((8,)),
        ],
        compiler_params=pltpu.CompilerParams(
            collective_id=1, has_side_effects=True, vmem_limit_bytes=38 << 20
        ),
        name="exchange",
    )(front, child_blocks, child_rows, child_cols, child_rows, child_cols, child_count)


def finish(mode, front_ref, recv_ref, lrh_ref, lrl_ref, lch_ref, lcl_ref, corner_ref, out_ref, add_ref, code_ref):
    i=pl.program_id(0)
    r=lax.axis_index("row") if "nomesh" not in mode else 3
    c=lax.axis_index("col") if "nomesh" not in mode else 3
    @pl.when(i==0)
    def _():
        for s in range(16):
            code_ref[s]=jnp.max(recv_ref[s,258:259,:]).astype(jnp.int32)
    add_ref[...]=jnp.zeros_like(add_ref)
    if "noch" not in mode:
        def slot(s,carry):
            code=code_ref[s]
            @pl.when((code>>3)==i)
            def _():
                rows=recv_ref[s,256:257,:].astype(jnp.int32)
                cols=recv_ref[s,257:258,:].astype(jnp.int32)
                t=lax.broadcasted_iota(jnp.int32,(256,256),0)
                R=jnp.where(rows==t,1.0,0.0).astype(BF)
                Q=jnp.where(cols==t,1.0,0.0).astype(BF)
                h,l=split(recv_ref[s,0:256,:])
                p=bdot(R,h,NN)+bdot(R,l,NN)
                h,l=split(p)
                j=code&7
                add_ref[j]=add_ref[j]+(bdot(h,Q,NT)+bdot(l,Q,NT))
            return carry
        lax.fori_loop(0,16,slot,0)
    special=jnp.logical_and(i==0,r<2)
    ah=lrh_ref[i]; al=lrl_ref[i]
    for j in range(8):
        bh=lch_ref[j]; bl=lcl_ref[j]
        if "noup" in mode: u=0.0
        else: u=bdot(ah,bh,NT)+(bdot(ah,bl,NT)+bdot(al,bh,NT))
        v=front_ref[0,:,j,:]+add_ref[j]-u
        out_ref[0,:,j,:]=v
    @pl.when(c<2)
    def _():
        @pl.when(c==0)
        def _(): out_ref[0,:,0,:]=ah[:,0:256].astype(F32)+al[:,0:256].astype(F32)
        @pl.when(c==1)
        def _(): out_ref[0,:,0,:]=ah[:,256:512].astype(F32)+al[:,256:512].astype(F32)
    @pl.when(special)
    def _():
        out_ref[0,:,1:8,:]=jnp.zeros((256,7,256),F32)
        out_ref[0,:,0,:]=corner_ref[...]
def kernel_b(mode,front,recv,lrh,lrl,lch,lcl,corner):
    return pl.pallas_call(functools.partial(finish,mode),grid=(4,),
        out_shape=jax.ShapeDtypeStruct((4,256,8,256),F32),
        in_specs=[pl.BlockSpec((1,256,8,256),lambda i:(i,0,0,0)),
                  *[pl.BlockSpec(memory_space=pltpu.VMEM)]*6],
        out_specs=pl.BlockSpec((1,256,8,256),lambda i:(i,0,0,0)),
        scratch_shapes=[pltpu.VMEM((8,256,256),F32),pltpu.SMEM((16,),jnp.int32)],
        compiler_params=pltpu.CompilerParams(vmem_limit_bytes=20<<20),name="finish_"+mode.replace(" ","_"))(front,recv,lrh,lrl,lch,lcl,corner)


def local(front, child_blocks, child_rows, child_cols, child_count):
    recv, lrh, lrl, lch, lcl, corner = exchange(front, child_blocks, child_rows, child_cols, child_count)
    return kernel_b("", front, recv, lrh, lrl, lch, lcl, corner)


def solution(mesh):
    placed = (
        P(None, "row", None, "col"),
        P(("row", "col"), None, None),
        P(("row", "col"), None),
        P(("row", "col"), None),
        P(("row", "col")),
    )
    return jax.shard_map(
        local, mesh=mesh, in_specs=placed, out_specs=P(None, "row", None, "col"), check_vma=False
    )
```

```python
import functools

import jax
import jax.numpy as jnp
from jax import lax
from jax.experimental import pallas as pl
from jax.experimental.pallas import tpu as pltpu
from jax.sharding import PartitionSpec as P

F32 = jnp.float32
BF = jnp.bfloat16
MESH = pl.DeviceIdType.MESH
TN = (((0,), (0,)), ((), ()))
NT = (((1,), (1,)), ((), ()))
NN = (((1,), (0,)), ((), ()))


def hdot(a, b, dn):
    return lax.dot_general(a, b, dn, precision=lax.Precision.HIGHEST, preferred_element_type=F32)


def bdot(a, b, dn):
    return lax.dot_general(a, b, dn, preferred_element_type=F32)


def split(x):
    hi = x.astype(BF)
    return hi, (x - hi.astype(F32)).astype(BF)


def factor(A, group=8, strip=32):
    ns = 128//strip
    lane = lax.broadcasted_iota(jnp.int32,(strip,128),1)
    sub = lax.broadcasted_iota(jnp.int32,(strip,128),0)
    def tile(J,carry):
        c0 = pl.multiple_of(J*128,128)
        for t in range(ns):
            r0 = pl.multiple_of(c0+strip*t,strip)
            S = [A[pl.ds(r0,strip),128*i:128*i+128] for i in range(4)]
            T = A[pl.ds(r0,strip),pl.ds(c0,128)]
            for s0 in range(0,strip,group):
                cols=[jnp.broadcast_to(T[:,strip*t+s0+a:strip*t+s0+a+1],(strip,128)) for a in range(group)]
                fs=[]
                for a in range(group):
                    s=s0+a
                    rd=1.0/cols[a][s:s+1,:]
                    f=jnp.where(sub>s,cols[a]*rd,0.0)
                    fs.append(f)
                    for b in range(a+1,group):
                        cols[b]=cols[b]-f*cols[b][s:s+1,:]
                for a in range(group):
                    s=s0+a; k=strip*t+s
                    f=fs[a]
                    rowT=jnp.where(lane[:1]==k,1.0,T[s:s+1,:])
                    T=jnp.where((lane==k)&(sub>s),0.0,T)-f*rowT
                    S=[x-f*x[s:s+1,:] for x in S]
            dg=(lane==sub+strip*t)
            d=jnp.sum(jnp.where(dg,T,0.0),axis=1,keepdims=True)
            rs=lax.rsqrt(d)
            rs=rs*(1.5-0.5*d*rs*rs)
            rs=jnp.broadcast_to(rs,(strip,128))
            T=jnp.where(dg,1.0,T)*rs
            for i in range(4): A[pl.ds(r0,strip),128*i:128*i+128]=S[i]*rs
            if t<ns-1:
                n=128-strip*(t+1)
                A[pl.ds(r0,strip),pl.ds(c0,128)]=jnp.where((lane>sub+strip*t)&(lane<strip*(t+1)),0.0,T)
                R=A[pl.ds(r0,strip),:]
                lm=jnp.where(lane>=strip*(t+1),T,0.0)
                upd=hdot(lm,R,TN)
                rb=pl.multiple_of(r0+strip,strip)
                lane_n=lax.broadcasted_iota(jnp.int32,(n,128),1)
                Tt=A[pl.ds(rb,n),pl.ds(c0,128)]
                A[pl.ds(rb,n),pl.ds(c0,128)]=jnp.where((lane_n>=strip*t)&(lane_n<strip*(t+1)),0.0,Tt)
                A[pl.ds(rb,n),:]=A[pl.ds(rb,n),:]-upd[strip*(t+1):]
            A[pl.ds(r0,strip),pl.ds(c0,128)]=T
        R=A[pl.ds(c0,128),:]
        D=A[pl.ds(c0,128),pl.ds(c0,128)]
        i1=lax.broadcasted_iota(jnp.int32,(128,128),1); i0=lax.broadcasted_iota(jnp.int32,(128,128),0)
        D=jnp.where(i1>i0,0.0,D)
        for m in range(1,4):
            @pl.when(m>J)
            def _(m=m):
                lm=A[pl.ds(c0,128),m*128:(m+1)*128]
                A[m*128:(m+1)*128,:]=A[m*128:(m+1)*128,:]-hdot(lm,R,TN)
                A[m*128:(m+1)*128,pl.ds(c0,128)]=-hdot(lm,D,TN)
        return carry
    lax.fori_loop(0,4,tile,0)


DQ = 2
YH = 4
CSTEP = 4
NH = 1


def m4(v):
    return lax.rem(v + 8, 4)


def comm_kernel(
    front, cb_in, crow, ccol, crow_s, ccol_s, cnt_s,
    recv, lrh, lrl, lch, lcl, corner,
    fbuf, pan, cb, lsem,
    stage, PR, PC, DG, AW, W3, LR,
    h1, h3, h4, h5, h6, y0s, y0r, y1s, y1r, ds, dr, dloc, xs_, xr_, cs, cr,
):
    r = lax.axis_index("row")
    c = lax.axis_index("col")
    z, x = r // 4, lax.rem(r, 4)
    y, k = c // 2, lax.rem(c, 2)
    zp, zm = jnp.where(z == 3, 0, z + 1), jnp.where(z == 0, 3, z - 1)
    xp, xm = jnp.where(x == 3, 0, x + 1), jnp.where(x == 0, 3, x - 1)
    yp, ym = jnp.where(y == 3, 0, y + 1), jnp.where(y == 0, 3, y - 1)

    def dev(z, x, y, k):
        return (z * 4 + x, y * 2 + k)

    other = dev(z, x, y, 1 - k)
    front_copies = [
        pltpu.make_async_copy(front.at[i], fbuf.at[i], lsem.at[i]) for i in range(4)
    ]
    cb_copy = pltpu.make_async_copy(cb_in, cb, lsem.at[4])

    @pl.when(y == 0)
    def _():
        for cp in front_copies:
            cp.start()

    cb_copy.start()

    b = pltpu.get_barrier_semaphore()
    for d in range(1, 8):
        pl.semaphore_signal(b, inc=1, device_id=(r, lax.rem(c + d, 8)), device_id_type=MESH)
    for s in (1, 3):
        pl.semaphore_signal(b, inc=1, device_id=dev(z, m4(x + s), y, k), device_id_type=MESH)
        pl.semaphore_signal(b, inc=1, device_id=dev(m4(z + s), x, y, k), device_id_type=MESH)
    pl.semaphore_wait(b, 11)

    def rcopy(src, dst, ss, rs, to):
        return pltpu.make_async_remote_copy(
            src_ref=src, dst_ref=dst, send_sem=ss, recv_sem=rs, device_id=to, device_id_type=MESH
        )

    def pack():
        owner = [lax.rem(ccol_s[s, 0] // 256, 8) for s in range(8)]
        live = [(s < cnt_s[0]).astype(jnp.int32) for s in range(8)]
        rank = []
        for s in range(8):
            n = jnp.int32(0)
            for q in range(s):
                n = n + live[q] * (owner[q] == owner[s]).astype(jnp.int32)
            rank.append(n)

        def slot(t, carry):
            idx = jnp.int32(0)
            ok = jnp.int32(0)
            for s in range(8):
                hit = live[s] * (owner[s] * 2 + rank[s] == t).astype(jnp.int32)
                idx = idx + hit * s
                ok = ok + hit
            rows = crow[pl.ds(idx, 1), :]
            cols = ccol[pl.ds(idx, 1), :]
            brow = rows // 4096
            bcol = cols // 2048
            code = jnp.where(ok > 0, brow * 8 + bcol, -1)
            stage[t, 0:256, :] = cb[idx]
            stage[t, 256:257, :] = lax.rem(rows, 256).astype(F32)
            stage[t, 257:258, :] = lax.rem(cols, 256).astype(F32)
            stage[t, 258:259, :] = code.astype(F32)
            stage[t, 259:264, :] = jnp.zeros((5, 256), F32)
            return carry

        lax.fori_loop(0, 16, slot, 0)

    def child_copy(d):
        to = lax.rem(c + d, 8)
        return rcopy(
            stage.at[pl.ds(to * 2, 2)], recv.at[pl.ds(c * 2, 2)], cs.at[d], cr.at[d], (r, to)
        )

    own_copy = pltpu.make_async_copy(stage.at[pl.ds(c * 2, 2)], recv.at[pl.ds(c * 2, 2)], cs.at[0])

    def start_children():
        own_copy.start()
        for d in (1, 7, 2, 6, 3, 5, 4):
            child_copy(d).start()

    def wait_children():
        own_copy.wait()
        for d in range(1, 8):
            child_copy(d).wait()

    def both(v):
        f = lax.rem(v + 4, 4)
        return f, jnp.where(f == 0, 0, 4 - f)

    def tree(oz, ox, xfirst, back1, back2, make):
        def pick(flag, a, b):
            if isinstance(flag, bool):
                return a if flag else b
            return jnp.where(flag, a, b)

        a = pick(xfirst, pick(back1, ox[1], ox[0]), pick(back1, oz[1], oz[0]))
        bb = pick(xfirst, pick(back2, oz[1], oz[0]), pick(back2, ox[1], ox[0]))
        row = z * 4 + x
        z_up, z_dn, x_up, x_dn = zp * 4 + x, zm * 4 + x, z * 4 + xp, z * 4 + xm
        up1, dn1 = pick(xfirst, x_up, z_up), pick(xfirst, x_dn, z_dn)
        up2, dn2 = pick(xfirst, z_up, x_up), pick(xfirst, z_dn, x_dn)
        is_src = a + bb == 0
        conds = (
            jnp.logical_and(bb == 0, a <= 1),
            is_src,
            bb <= 1,
            bb == 0,
        )
        targets = (
            (pick(back1, dn1, up1), c), (pick(back1, up1, dn1), c),
            (pick(back2, dn2, up2), c), (pick(back2, up2, dn2), c),
        )
        copies = [make(e, to) for e, to in enumerate(targets)]
        return is_src, conds, copies

    h1_copies = [
        rcopy(pan.at[i], PR.at[2 * i + 1], h1.at[i, 0], h1.at[i, 1], other) for i in range(4)
    ]
    h3_copy = rcopy(AW, AW, h3.at[0], h3.at[1], other)

    def h4_copy(j):
        return rcopy(PR.at[j], PR.at[j], h4.at[j, 0], h4.at[j, 1], other)

    y_depth = (y, jnp.where(y == 0, 0, 4 - y))
    y_next = (dev(z, x, yp, k), dev(z, x, ym, k))

    def y1_part(br, p, h):
        rows = pl.ds(h * (256 // YH), 256 // YH)
        ref = PR.at[2 * br + p, rows]
        j = (2 * br + p) * YH + h
        return rcopy(ref, ref, y1s.at[j], y1r.at[j], y_next[p])

    def h5_copy(i, src, h):
        ref = PC.at[2 * src, i, pl.ds(h * (256 // NH), 256 // NH)]
        j = (2 * i + src) * NH + h
        return rcopy(ref, ref, h5.at[j, 0], h5.at[j, 1], other)

    def y0_parts(j):
        p, qt = j // DQ, j % DQ
        ref = PR.at[p, pl.ds(qt * (256 // DQ), 256 // DQ)]
        fwd = rcopy(ref, ref, y0s.at[j, 0], y0r.at[j], y_next[p])
        back = rcopy(ref, ref, y0s.at[j, 1], y0r.at[j], y_next[1 - p])
        return p, y_depth[p], fwd, back

    dz_ = both(z)
    dx_ = (both(x), both(x - 1))

    def d_parts(j):
        d, qt = j // DQ, j % DQ
        rows = pl.ds(qt * (256 // DQ), 256 // DQ)
        ref = DG.at[d, rows]
        back = d % 2 == 1
        parts = tree(
            dz_, dx_[min(d, 1)], True, back, back,
            lambda e, to: rcopy(ref, ref, ds.at[j, e], dr.at[j], to),
        )
        return parts, d, rows

    def d_sources(p, qt):
        for row in (0, 1) if p == 0 else (1,):
            @pl.when(r == row)
            def _(row=row):
                d = row + p
                (is_src, conds, copies), d, rows = d_parts(d * DQ + qt)
                DG[d, rows, :] = PR[p, rows, :]
                for cp in copies:
                    cp.start()

    i0 = lax.broadcasted_iota(jnp.int32, (256, 256), 0)
    i1 = lax.broadcasted_iota(jnp.int32, (256, 256), 1)
    low = i1 <= i0
    def prepare():
        for n, w in enumerate((
            jnp.where(low, AW[0:256, 0:256], 0.0),
            AW[256:512, 0:256],
            jnp.where(low, AW[256:512, 256:512], 0.0),
        )):
            hi, lo = split(w)
            W3[n, :, 0:256], W3[n, :, 256:512], W3[n, :, 512:768] = hi, lo, hi

    def times_w(a3, w):
        return bdot(a3, W3[w], NT)

    def solve(m0, m1, put):
        h, l = split(m0)
        a0 = jnp.concatenate([h, h, l], axis=1)
        h, l = split(m1)
        a1 = jnp.concatenate([h, h, l], axis=1)
        put(0, times_w(a0, 0))
        put(1, times_w(a0, 1) + times_w(a1, 2))

    def row_solve(i, carry):
        def put(p, v):
            cols = pl.ds(p * 256, 256)
            LR[i, :, cols] = v
            lrh[i, :, cols], lrl[i, :, cols] = split(v)

        solve(PR[2 * i], PR[2 * i + 1], put)
        return carry


    def col_solve(i, carry):
        def put(p, v):
            cols = pl.ds(p * 256, 256)
            lch[i, :, cols], lcl[i, :, cols] = split(v)

        row_set, j = k + 2 * lax.rem(i, 2), 2 * (i // 2)
        solve(PC[row_set, j], PC[row_set, j + 1], put)
        return carry

    lr_copy = rcopy(LR, LR, h6.at[0], h6.at[1], other)

    @pl.when(k == 0)
    def _():
        @pl.when(y == 0)
        def _():
            for i in range(4):
                front_copies[i].wait()
                PR[2 * i] = fbuf[i, :, 0, :]
            for cp in h1_copies:
                cp.wait_recv()

        for j in range(2 * DQ):
            p, yy, fwd, back = y0_parts(j)

            @pl.when(yy != 0)
            def _():
                fwd.wait_recv()

            @pl.when(yy <= 1)
            def _():
                fwd.start()

            @pl.when(yy == 0)
            def _():
                back.start()

            if j % DQ == DQ - 1:
                h4_copy(p).start()
            d_sources(p, j % DQ)

        def y1_step(t, carry):
            for h in range(YH):
                for p in range(2):
                    yy = y_depth[p]
                    br = t - yy

                    @pl.when(jnp.logical_and(br >= 1, br <= 3))
                    def _(p=p, yy=yy, br=br, h=h):
                        fwd = y1_part(br, p, h)

                        @pl.when(yy != 0)
                        def _():
                            fwd.wait_recv()

                        @pl.when(yy < 3)
                        def _():
                            fwd.start()

                        if h == YH - 1:
                            h4_copy(2 * br + p).start()

            return carry

        lax.fori_loop(1, 7, y1_step, 0)

        for j in range(3 * DQ):
            (is_src, conds, copies), d, rows = d_parts(j)

            @pl.when(jnp.logical_not(is_src))
            def _():
                copies[0].wait_recv()
                for cond, cp in zip(conds, copies):
                    @pl.when(cond)
                    def _(cp=cp):
                        cp.start()

        cb_copy.wait()
        pack()
        start_children()

        AW[0:256, 0:256] = (DG[0] + DG[0].T) * 0.5
        AW[0:256, 256:512] = DG[1].T
        AW[256:512, 0:256] = jnp.zeros((256, 256), F32)
        AW[256:512, 256:512] = (DG[2] + DG[2].T) * 0.5
        factor(AW)
        h3_copy.start()

        prepare()
        lax.fori_loop(0, 4, row_solve, 0)
        lr_copy.start()

        def col_pair(br, carry):
            for i in range(2):
                for src in range(2):
                    for h in range(NH):
                        h5_copy(2 * br + i, src, h).wait_recv()
            for src in range(2):
                col_solve(2 * br + src, 0)
            return carry

        lax.fori_loop(0, 4, col_pair, 0)

    xz_off = []
    xz_depth = []
    for s in range(4):
        row = 2 * y + s % 2 + 8 * (s // 2)
        oz, ox = both(z - row // 4), both(x - lax.rem(row, 4))
        xz_off.append((oz, ox))
        xz_depth.append(jnp.minimum(oz[0], oz[1]) + jnp.minimum(ox[0], ox[1]))

    def xz_parts(i, s, h):
        ref = PC.at[s, i, pl.ds(h * (256 // NH), 256 // NH)]
        zfirst = jnp.logical_or(i == 3, i == 7)
        back1 = i >= 4
        back2 = jnp.logical_or(jnp.logical_or(i == 1, i == 3), jnp.logical_or(i == 4, i == 6))
        q = (4 * i + s) * NH + h
        oz, ox = xz_off[s]
        return tree(
            oz, ox, jnp.logical_not(zfirst), back1, back2,
            lambda e, to: rcopy(ref, ref, xs_.at[q, e], xr_.at[q], to),
        )

    @pl.when(k == 1)
    def _():
        @pl.when(y == 0)
        def _():
            for i in range(4):
                front_copies[i].wait()
                pan[i] = fbuf[i, :, 0, :]
                h1_copies[i].start()

        cb_copy.wait()
        pack()

        def xz_step(t, carry):
            for h in range(NH):
                for s in range(4):
                    dep = xz_depth[s]
                    i = t - dep

                    @pl.when(jnp.logical_and(i >= 0, i < 8))
                    def _(s=s, dep=dep, i=i, h=h):
                        _, conds, copies = xz_parts(i, s, h)

                        @pl.when(dep == 0)
                        def _():
                            if h == 0:
                                h4_copy(i).wait_recv()
                                PC[s, i] = PR[i]

                        @pl.when(dep != 0)
                        def _():
                            copies[0].wait_recv()

                        for cond, cp in zip(conds, copies):
                            @pl.when(cond)
                            def _(cp=cp):
                                cp.start()

                        if s % 2 == 0:
                            h5_copy(i, s // 2, h).start()

            return carry

        lax.fori_loop(0, CSTEP, xz_step, 0)
        start_children()
        lax.fori_loop(CSTEP, 11, xz_step, 0)
        h3_copy.wait_recv()
        prepare()
        lax.fori_loop(0, 4, col_solve, 0)
        lax.fori_loop(11, 12, xz_step, 0)

        def h4_wait(j, carry):
            h4_copy(j).wait_recv()
            return carry

        @pl.when(lax.rem(r, 8) // 2 != y)
        def _():
            lax.fori_loop(0, 8, h4_wait, 0)

        lax.fori_loop(4, 8, col_solve, 0)
        lr_copy.wait_recv()
        for i in range(4):
            lrh[i], lrl[i] = split(LR[i])

    corner[...] = jnp.zeros((256, 256), F32)

    def diag_block(o):
        t = AW[o : o + 256, o : o + 256].T
        return jnp.where(i1 < i0, t, jnp.where(i1 == i0, 1.0 / t, 0.0))

    @pl.when(jnp.logical_and(r == 0, c == 0))
    def _():
        corner[...] = diag_block(0)

    @pl.when(jnp.logical_and(r == 1, c == 0))
    def _():
        corner[...] = AW[0:256, 256:512].T

    @pl.when(jnp.logical_and(r == 1, c == 1))
    def _():
        corner[...] = diag_block(256)

    @pl.when(k == 0)
    def _():
        for j in range(2 * DQ):
            p, yy, fwd, back = y0_parts(j)

            @pl.when(yy <= 1)
            def _():
                fwd.wait_send()

            @pl.when(yy == 0)
            def _():
                back.wait_send()

        def y1_end(br, carry):
            for p in range(2):
                @pl.when(y_depth[p] < 3)
                def _(p=p):
                    for h in range(YH):
                        y1_part(br, p, h).wait_send()

            return carry

        lax.fori_loop(1, 4, y1_end, 0)

        def h4_end(j, carry):
            h4_copy(j).wait_send()
            return carry

        lax.fori_loop(0, 8, h4_end, 0)

        for j in range(3 * DQ):
            (is_src, conds, copies), d, rows = d_parts(j)
            for cond, cp in zip(conds, copies):
                @pl.when(cond)
                def _(cp=cp):
                    cp.wait_send()

        h3_copy.wait_send()
        lr_copy.wait_send()

    @pl.when(k == 1)
    def _():
        @pl.when(y == 0)
        def _():
            for cp in h1_copies:
                cp.wait_send()

        def xz_end(i, carry):
            for s in range(4):
                for h in range(NH):
                    _, conds, copies = xz_parts(i, s, h)
                    for cond, cp in zip(conds, copies):
                        @pl.when(cond)
                        def _(cp=cp):
                            cp.wait_send()

                    if s % 2 == 0:
                        h5_copy(i, s // 2, h).wait_send()

            return carry

        lax.fori_loop(0, 8, xz_end, 0)

    wait_children()


def exchange(front, child_blocks, child_rows, child_cols, child_count):
    vm = pl.BlockSpec(memory_space=pltpu.VMEM)
    sm = pl.BlockSpec(memory_space=pltpu.SMEM)
    hbm = pl.BlockSpec(memory_space=pltpu.HBM)
    dma = pltpu.SemaphoreType.DMA
    return pl.pallas_call(
        comm_kernel,
        out_shape=(
            jax.ShapeDtypeStruct((16, 264, 256), F32),
            jax.ShapeDtypeStruct((4, 256, 512), BF),
            jax.ShapeDtypeStruct((4, 256, 512), BF),
            jax.ShapeDtypeStruct((8, 256, 512), BF),
            jax.ShapeDtypeStruct((8, 256, 512), BF),
            jax.ShapeDtypeStruct((256, 256), F32),
        ),
        in_specs=[hbm, hbm, vm, vm, sm, sm, sm],
        out_specs=(vm, vm, vm, vm, vm, vm),
        scratch_shapes=[
            pltpu.VMEM((4, 256, 8, 256), F32),
            pltpu.VMEM((4, 256, 256), F32),
            pltpu.VMEM((8, 256, 256), F32),
            dma((5,)),
            pltpu.VMEM((16, 264, 256), F32),
            pltpu.VMEM((8, 256, 256), F32),
            pltpu.VMEM((4, 8, 256, 256), F32),
            pltpu.VMEM((3, 256, 256), F32),
            pltpu.VMEM((512, 512), F32),
            pltpu.VMEM((3, 256, 768), BF),
            pltpu.VMEM((4, 256, 512), F32),
            dma((4, 2)), dma((2,)), dma((8, 2)), dma((16 * NH, 2)), dma((2,)),
            dma((8, 2)), dma((8,)), dma((8 * YH,)), dma((8 * YH,)),
            dma((12, 4)), dma((12,)), dma, dma((32 * NH, 4)), dma((32 * NH,)),
            dma((8,)), dma((8,)),
        ],
        compiler_params=pltpu.CompilerParams(
            collective_id=1, has_side_effects=True, vmem_limit_bytes=38 << 20
        ),
        name="exchange",
    )(front, child_blocks, child_rows, child_cols, child_rows, child_cols, child_count)


def finish(mode, front_ref, recv_ref, lrh_ref, lrl_ref, lch_ref, lcl_ref, corner_ref, out_ref, code_ref):
    i=pl.program_id(0)
    r=lax.axis_index("row") if "nomesh" not in mode else 3
    c=lax.axis_index("col") if "nomesh" not in mode else 3
    @pl.when(i==0)
    def _():
        for s in range(16):
            code_ref[s]=jnp.max(recv_ref[s,258:259,:]).astype(jnp.int32)
    special=jnp.logical_and(i==0,r<2)
    ah=lrh_ref[i]; al=lrl_ref[i]
    a3=jnp.concatenate([ah,ah,al],axis=1)
    for j in range(8):
        bh=lch_ref[j]; bl=lcl_ref[j]
        u=bdot(a3,jnp.concatenate([bh,bl,bh],axis=1),NT)
        out_ref[0,:,j,:]=front_ref[0,:,j,:]-u
    if "noch" not in mode:
        def slot(s,carry):
            code=code_ref[s]
            @pl.when((code>>3)==i)
            def _():
                rows=recv_ref[s,256:257,:].astype(jnp.int32)
                cols=recv_ref[s,257:258,:].astype(jnp.int32)
                t=lax.broadcasted_iota(jnp.int32,(256,256),0)
                R=jnp.where(rows==t,1.0,0.0).astype(BF)
                Q=jnp.where(cols==t,1.0,0.0).astype(BF)
                h,l=split(recv_ref[s,0:256,:])
                p=bdot(R,h,NN)+bdot(R,l,NN)
                h,l=split(p)
                p=bdot(h,Q,NT)+bdot(l,Q,NT)
                for j in range(8):
                    @pl.when((code&7)==j)
                    def _(j=j):
                        out_ref[0,:,j,:]=out_ref[0,:,j,:]+p
            return carry
        lax.fori_loop(0,16,slot,0)
    @pl.when(c<2)
    def _():
        @pl.when(c==0)
        def _(): out_ref[0,:,0,:]=ah[:,0:256].astype(F32)+al[:,0:256].astype(F32)
        @pl.when(c==1)
        def _(): out_ref[0,:,0,:]=ah[:,256:512].astype(F32)+al[:,256:512].astype(F32)
    @pl.when(special)
    def _():
        out_ref[0,:,1:8,:]=jnp.zeros((256,7,256),F32)
        out_ref[0,:,0,:]=corner_ref[...]
def kernel_b(mode,front,recv,lrh,lrl,lch,lcl,corner):
    return pl.pallas_call(functools.partial(finish,mode),grid=(4,),
        out_shape=jax.ShapeDtypeStruct((4,256,8,256),F32),
        in_specs=[pl.BlockSpec((1,256,8,256),lambda i:(i,0,0,0)),
                  *[pl.BlockSpec(memory_space=pltpu.VMEM)]*6],
        out_specs=pl.BlockSpec((1,256,8,256),lambda i:(i,0,0,0)),
        scratch_shapes=[pltpu.SMEM((16,),jnp.int32)],
        compiler_params=pltpu.CompilerParams(vmem_limit_bytes=20<<20),name="finish_"+mode.replace(" ","_"))(front,recv,lrh,lrl,lch,lcl,corner)


def local(front, child_blocks, child_rows, child_cols, child_count):
    recv, lrh, lrl, lch, lcl, corner = exchange(front, child_blocks, child_rows, child_cols, child_count)
    return kernel_b("", front, recv, lrh, lrl, lch, lcl, corner)


def solution(mesh):
    placed = (
        P(None, "row", None, "col"),
        P(("row", "col"), None, None),
        P(("row", "col"), None),
        P(("row", "col"), None),
        P(("row", "col")),
    )
    return jax.shard_map(
        local, mesh=mesh, in_specs=placed, out_specs=P(None, "row", None, "col"), check_vma=False
    )
```
